128 devices in a mesh: grp: 32 (over z, y, x_hi), ep: 2 (over core), tp: 2 (over x_lo).
Axes of the slice: x: 4 (x_hi: 2, x_lo: 2; x = x_hi * 2 + x_lo), y: 4, z: 4, core: 2. Of those that a mesh axis runs over, the one named last changes fastest.
Arguments:
- queries: bfloat16 [3, 32, 6144], P(None, 'grp', 'ep')
- new_keys: bfloat16 [3, 32, 1024], P(None, 'grp', 'ep'), may hold values from -6 to 6
- new_values: bfloat16 [3, 32, 1024], P(None, 'grp', 'ep'), may hold values from -6 to 6
- cache_keys: bfloat16 [32, 1024, 1024], P('grp', 'tp', 'ep')
- cache_values: bfloat16 [32, 1024, 1024], P('grp', 'tp', 'ep'), may hold values from -6 to 6
- lengths: int32 [32], P('grp'), may hold values from 2 to 1024, as said below
- residual: bfloat16 [3, 32, 6144], P(None, 'grp', 'tp'), may hold values from -6 to 6
- out_weight: bfloat16 [6144, 6144], P('ep', 'tp'), may hold values from -0.078125 to 0.078125
- norm_gain: float32 [6144], P('tp'), may hold values from 0.1 to 1.9
- router_weight: bfloat16 [6144, 8], P('tp'), may hold values from -0.078125 to 0.078125
- routes: int32 [3, 32, 2], replicated, may hold values from 0 to 7, all different within a row; in each aligned block of 96 rows (0 to 95, 96 to 191, ..., all dimensions but the last counted through in order) at most 48 rows name the same one
- expert_gate: bfloat16 [8, 6144, 8192], P('ep', 'tp', 'grp'), may hold values from -0.078125 to 0.078125
- expert_up: bfloat16 [8, 6144, 8192], P('ep', 'tp', 'grp'), may hold values from -0.078125 to 0.078125
- expert_down: bfloat16 [8, 8192, 6144], P('ep', 'grp', 'tp'), may hold values from -0.0625 to 0.0625
Outputs:
- mixed: bfloat16 [3, 32, 6144], P(None, 'grp', 'tp')
The draws below stay inside these ranges and needn't reach their ends.
Inputs may be any that keep to these rules, and one draw needn't show every extreme that they name: `lengths`: one sequence has exactly 1024 valid positions. `routes`: the two experts of a token differ, every expert is named by some token, and over all 96 tokens no expert is named by more than 48 of them; one expert is named by exactly 48.
All inputs are finite; a program needn't handle non-finite values.
Results may differ from the reference program's by a relative error of at most 0.02.
Values may be sent and summed in bfloat16 or wider, within the bound.
No kernel may reach another device: no remote copies, remote signals or barrier semaphores. Data moves between devices by JAX's collectives and lax.ppermute only.
A program may use at most 128 MiB of HBM per device.

```python
import math
import jax
import jax.numpy as jnp
import numpy as np
from jax import lax

D = 6144
HEADS = 48
KV = 8
HD = 128
E = 8
FF = 8192
STEPS = 3
SEQS = 32
CACHE = 1024
CAP = 48


def shared_queries(key):
    return jax.random.normal(key, (STEPS, SEQS, HEADS * HD), jnp.float32)


def draw_queries(key, part):
    base = shared_queries(key)
    return base.astype(jnp.bfloat16)


def draw_cache_keys(key, part):
    key = jax.random.fold_in(key, 12)
    noise = jax.random.normal(key, (SEQS, CACHE, KV * HD), jnp.float32)
    return noise.astype(jnp.bfloat16)


def draw_lengths(key, part):
    key = jax.random.fold_in(key, 13)
    draw_key, pick_key = jax.random.split(key)
    drawn = jax.random.randint(draw_key, (SEQS,), 2, CACHE + 1)
    longest = jax.random.randint(pick_key, (), 0, SEQS)
    return jnp.where(jnp.arange(SEQS) == longest, CACHE, drawn).astype(jnp.int32)


def steps_of(stream_key, dims, cuts, smallest, high):
    def one(dim, shards_of):
        steps = jax.random.uniform(jax.random.fold_in(jax.random.fold_in(stream_key, 6), dim), (shards_of,), jnp.float32, smallest / len(cuts), high / len(cuts))
        return jnp.repeat(jnp.exp(steps), dims[dim] // shards_of).reshape((-1,) + (1,) * (len(dims) - dim - 1))

    level = one(*cuts[0])
    for cut in cuts[1:]:
        level = level * one(*cut)
    return level


def routed_block(key, own, number, rows, number_of, top, limit, skew):
    sequence = jax.random.permutation(key, number_of)
    heavy_load, common = portions_of(number_of, rows * top, limit, skew, True), portions_of(number_of, rows * top, limit, skew, False)
    places = jnp.arange(number_of)

    def named(tallies, turn):
        used = int((tallies > 0).sum())
        fixed = max(1, used // 4)
        moved = fixed + (places - fixed + turn * (used - fixed)) % max(1, number_of - fixed)
        return jnp.zeros((number_of,), jnp.int32).at[sequence[jnp.where(places < fixed, places, moved)]].set(jnp.asarray(tallies, jnp.int32))

    tallies = jnp.where(number % 4 == 0, named(heavy_load, number // 4), named(common, number - number // 4 - 1))
    mixed = jax.random.permutation(jax.random.fold_in(own, 3), number_of)
    donor, taker = mixed[0:number_of // 2 * 2:2], mixed[1:number_of // 2 * 2:2]
    slack = jnp.minimum(tallies[donor] - 1, limit - tallies[taker]) // 2
    slack = jnp.where((donor == sequence[0]) | (taker == sequence[0]) | (tallies[taker] == 0), 0, jnp.maximum(slack, 0))
    moved = jax.random.randint(jax.random.fold_in(own, 4), (number_of // 2,), 0, 1 << 20) % (slack + 1)
    tallies = tallies.at[donor].add(-moved).at[taker].add(moved)
    members = jnp.searchsorted(jnp.cumsum(tallies), jnp.arange(rows * top), side="right").astype(jnp.int32)
    listing = members.reshape(top, rows).T
    listing = listing[jax.random.permutation(jax.random.fold_in(own, 1), rows)]
    turn = jax.random.randint(jax.random.fold_in(own, 2), (rows, 1), 0, top)
    return jnp.take_along_axis(listing, (jnp.arange(top)[None, :] + turn) % top, axis=1)


def portions_of(amount, total, most, skew, full):
    loads = [(1 << 20) // math.isqrt(rank ** skew) + 1 for rank in range(1, amount + 1)]
    largest = most if full else min(most, max(-(-total // amount), total * loads[0] // sum(loads)))
    least = 1 if total - largest >= amount - 1 else 0
    counts, rest = [largest] + [least] * (amount - 1), total - largest - least * (amount - 1)
    while rest > 0:
        candidates = [i for i in range(1, amount) if counts[i] < largest] or [i for i in range(1, amount) if counts[i] < most]
        mass, budget = sum([loads[i] for i in candidates]), rest
        for i in candidates:
            addition = min(most - counts[i], max(1, budget * loads[i] // mass), rest)
            counts[i] = counts[i] + addition
            rest = rest - addition
    return np.array(counts)


def scatter_about(key, shape, spread, limit, shards=(), kind=jnp.bfloat16):
    loudness = steps_of(key, shape, shards, -0.22, 0.18) if shards else 1.0
    values = jax.random.normal(key, shape, jnp.float32) * spread * loudness
    return jnp.minimum(jnp.maximum(values, -limit), limit).astype(kind)


def setup_inputs(seed: int = 0) -> dict:
    splits = jax.random.split(jax.random.key(seed), 15)
    queries = draw_queries(jax.random.fold_in(splits[14], 71), 0)
    new_keys = scatter_about(splits[1], (STEPS, SEQS, KV * HD), 1.0, 6.0, ((1, 32), (2, 2)))
    new_values = scatter_about(splits[2], (STEPS, SEQS, KV * HD), 1.0, 6.0, ((1, 32), (2, 2)))
    cache_keys = draw_cache_keys(jax.random.fold_in(splits[14], 71), 0)
    cache_values = scatter_about(splits[4], (SEQS, CACHE, KV * HD), 1.0, 6.0, ((0, 32), (1, 2), (2, 2)))
    lengths = draw_lengths(jax.random.fold_in(splits[14], 71), 0)
    residual = scatter_about(splits[6], (STEPS, SEQS, D), 1.0, 6.0, ((1, 32), (2, 2)))
    out_weight = scatter_about(splits[7], (HEADS * HD, D), (HEADS * HD) ** -0.5, 0.078125, ((0, 2), (1, 2)))
    norm_gain = jnp.clip(1.0 + 0.18 * jax.random.normal(splits[8], (D,), jnp.float32), 0.1, 1.9)
    router_weight = scatter_about(splits[9], (D, E), D ** -0.5, 0.078125, ((0, 2),))
    routes_keys = jax.random.split(jax.random.fold_in(splits[10], 1), STEPS * SEQS // (STEPS * SEQS))
    routes_turns = jax.random.permutation(jax.random.fold_in(splits[10], 3), STEPS * SEQS // (STEPS * SEQS))
    routes = jax.vmap(lambda own, number: routed_block(jax.random.fold_in(splits[10], 2), own, number, STEPS * SEQS, E, 2, CAP, 1))(routes_keys, routes_turns).reshape((STEPS, SEQS, 2))
    expert_gate = scatter_about(splits[11], (E, D, FF), D ** -0.5, 0.078125, ((0, 2), (1, 2), (2, 32)))
    expert_up = scatter_about(splits[12], (E, D, FF), D ** -0.5, 0.078125, ((0, 2), (1, 2), (2, 32)))
    expert_down = scatter_about(splits[13], (E, FF, D), FF ** -0.5, 0.0625, ((0, 2), (1, 32), (2, 2)))
    return dict(queries=queries, new_keys=new_keys, new_values=new_values, cache_keys=cache_keys, cache_values=cache_values, lengths=lengths, residual=residual, out_weight=out_weight, norm_gain=norm_gain, router_weight=router_weight, routes=routes, expert_gate=expert_gate, expert_up=expert_up, expert_down=expert_down)


far_below = -1e+30
epsilon = 1e-05

def reference(queries, new_keys, new_values, cache_keys, cache_values, lengths, residual, out_weight, norm_gain, router_weight, routes, expert_gate, expert_up, expert_down):
    group_size = HEADS // KV
    scale = HD ** (-0.5)
    query_heads = queries.astype(jnp.float32).reshape(STEPS, SEQS, KV, group_size, HD)
    cache_key = cache_keys.astype(jnp.float32).reshape(SEQS, CACHE, KV, HD)
    cache_value = cache_values.astype(jnp.float32).reshape(SEQS, CACHE, KV, HD)
    fresh_key = new_keys.astype(jnp.float32).reshape(STEPS, SEQS, KV, HD)
    fresh_value = new_values.astype(jnp.float32).reshape(STEPS, SEQS, KV, HD)
    stored_ok = (jnp.arange(CACHE, dtype=jnp.int32)[None, :] < lengths[:, None])[None, :, None, None, :]
    stored_scores = jnp.einsum('sbkgd,bpkd->sbkgp', query_heads, cache_key) * scale
    stored_scores = jnp.where(stored_ok, stored_scores, far_below)
    order = jnp.arange(STEPS, dtype=jnp.int32)
    fresh_ok = (order[:, None] >= order[None, :])[:, None, None, None, :]
    fresh_scores = jnp.einsum('sbkgd,tbkd->sbkgt', query_heads, fresh_key) * scale
    fresh_scores = jnp.where(fresh_ok, fresh_scores, far_below)
    highest = jnp.maximum(lax.optimization_barrier(jnp.max(stored_scores, axis=-1)), lax.optimization_barrier(jnp.max(fresh_scores, axis=-1)))
    stored_exp = jnp.where(stored_ok, jnp.exp(stored_scores - highest[..., None]), 0.0)
    fresh_exp = jnp.where(fresh_ok, jnp.exp(fresh_scores - highest[..., None]), 0.0)
    totals = lax.optimization_barrier(jnp.sum(stored_exp, axis=-1)) + lax.optimization_barrier(jnp.sum(fresh_exp, axis=-1))
    stored_round = lax.optimization_barrier(stored_exp.astype(jnp.bfloat16)).astype(jnp.float32)
    fresh_round = lax.optimization_barrier(fresh_exp.astype(jnp.bfloat16)).astype(jnp.float32)
    weighted = jnp.einsum('sbkgp,bpkd->sbkgd', stored_round, cache_value) + jnp.einsum('sbkgt,tbkd->sbkgd', fresh_round, fresh_value)
    attended = (weighted / totals[..., None]).astype(jnp.bfloat16).reshape(STEPS * SEQS, HEADS * HD)
    attn_out = jnp.dot(attended, out_weight, preferred_element_type=jnp.float32)
    state = (residual.reshape(STEPS * SEQS, D).astype(jnp.float32) + attn_out).astype(jnp.bfloat16)
    state_wide = state.astype(jnp.float32)
    inverse = lax.rsqrt(lax.optimization_barrier(jnp.mean(state_wide * state_wide, axis=-1)) + epsilon)
    scaled = (state_wide * norm_gain).astype(jnp.bfloat16)
    logits = jnp.dot(scaled, router_weight, preferred_element_type=jnp.float32) * inverse[:, None]
    chosen = routes.reshape(STEPS * SEQS, 2)
    choose_table = (chosen[:, :, None] == jnp.arange(E, dtype=jnp.int32)[None, None, :]).astype(jnp.float32)
    picked = lax.optimization_barrier(jnp.sum(logits[:, None, :] * choose_table, axis=-1))
    shares = jax.nn.softmax(picked, axis=-1)
    expert_share = lax.optimization_barrier(jnp.sum(shares[:, :, None] * choose_table, axis=1))

    def one_expert(carry, index):
        gate = jnp.dot(scaled, expert_gate[index], preferred_element_type=jnp.float32) * inverse[:, None]
        upward = jnp.dot(scaled, expert_up[index], preferred_element_type=jnp.float32) * inverse[:, None]
        activated = (jax.nn.silu(gate) * upward).astype(jnp.bfloat16)
        downward = jnp.dot(activated, expert_down[index], preferred_element_type=jnp.float32)
        picked_share = lax.optimization_barrier(jnp.sum(expert_share * (jnp.arange(E, dtype=jnp.int32) == index).astype(jnp.float32)[None, :], axis=1))
        return (carry + picked_share[:, None] * downward, None)
    moe, unused = lax.scan(one_expert, jnp.zeros((STEPS * SEQS, D), jnp.float32), jnp.arange(E, dtype=jnp.int32))
    mixed = (state_wide + moe).astype(jnp.bfloat16)
    return mixed.reshape(STEPS, SEQS, D)
```

```python
import functools

import jax
import jax.numpy as jnp
from jax import lax
from jax.experimental import pallas as pl
from jax.experimental.pallas import tpu as pltpu
from jax.sharding import PartitionSpec as P

D = 6144
HD = 128
E = 8
CAP = 48
LANES = 128

far_below = -1e30
epsilon = 1e-05
VMEM = pl.BlockSpec(memory_space=pltpu.VMEM)
SMEM = pl.BlockSpec(memory_space=pltpu.SMEM)
swap = [(0, 1), (1, 0)]
f32 = jnp.float32
bf16 = jnp.bfloat16


def call(kernel, out, operands, specs, scratch=(), limit=16):
    return pl.pallas_call(
        kernel,
        out_shape=out,
        in_specs=specs,
        out_specs=jax.tree.map(lambda _: VMEM, out),
        scratch_shapes=scratch,
        compiler_params=pltpu.CompilerParams(vmem_limit_bytes=limit * 2**20),
    )(*operands)


def iota(shape, dim):
    return lax.broadcasted_iota(jnp.int32, shape, dim)


def pieces(value):
    high = value.astype(bf16).astype(f32)
    rest = value - high
    middle = rest.astype(bf16).astype(f32)
    return high, middle, rest - middle


def attention_kernel(
    length_ref, query_ref, key_ref, value_ref, new_key_ref, new_value_ref, out_ref, rows_ref
):
    steps = query_ref.shape[0]
    heads = query_ref.shape[1] // HD
    kv = key_ref.shape[1] // HD
    cached = key_ref.shape[0]
    rows = heads * steps
    per_kv = rows // kv
    part = lax.axis_index("tp")
    for h in range(heads):
        rows_ref[h * steps : (h + 1) * steps, :] = query_ref[:, h * HD : (h + 1) * HD].astype(f32)
    query = rows_ref[...]
    row = iota((rows, 1), 0)
    owner = [(row >= k * per_kv) & (row < (k + 1) * per_kv) for k in range(kv)]
    step = row % steps
    scale = HD ** (-0.5)
    spread = jnp.concatenate(
        [jnp.where(owner[k], query, 0.0).astype(bf16) for k in range(kv)], axis=1
    )
    scores = (
        lax.dot_general(
            spread, key_ref[...], (((1,), (1,)), ((), ())), preferred_element_type=f32
        )
        * scale
    )
    allowed = (iota((1, cached), 1) + part * cached) < length_ref[0]
    scores = jnp.where(allowed, scores, far_below)
    new_key = new_key_ref[...].astype(f32)
    new_value = new_value_ref[...].astype(f32)

    def chosen(wide, t):
        out = jnp.zeros((rows, HD), f32)
        for k in range(kv):
            out = jnp.where(owner[k], wide[t : t + 1, k * HD : (k + 1) * HD], out)
        return out

    fresh_ok = [(step >= t) & (part == 0) for t in range(steps)]
    fresh = [
        jnp.where(
            fresh_ok[t],
            jnp.sum(query * chosen(new_key, t), axis=1, keepdims=True) * scale,
            far_below,
        )
        for t in range(steps)
    ]
    highest = jnp.max(scores, axis=1, keepdims=True)
    for t in range(steps):
        highest = jnp.maximum(highest, fresh[t])
    exponent = jnp.where(allowed, jnp.exp(scores - highest), 0.0)
    totals = jnp.sum(exponent, axis=1, keepdims=True)
    wide = jnp.dot(exponent.astype(bf16), value_ref[...], preferred_element_type=f32)
    weighted = jnp.zeros((rows, HD), f32)
    for k in range(kv):
        weighted = jnp.where(owner[k], wide[:, k * HD : (k + 1) * HD], weighted)
    for t in range(steps):
        term = jnp.where(fresh_ok[t], jnp.exp(fresh[t] - highest), 0.0)
        totals = totals + term
        weighted = weighted + term.astype(bf16).astype(f32) * chosen(new_value, t)
    present = totals > 0.0
    safe = jnp.where(present, totals, 1.0)
    out_ref[:, :HD] = (weighted / safe).astype(bf16)
    level = jnp.where(present, highest + jnp.log(safe), far_below)
    high, middle, low = pieces(level)
    lane = iota((rows, LANES), 1)
    out_ref[:, HD:] = jnp.where(lane == 0, high, jnp.where(lane == 1, middle, low)).astype(bf16)


def project_kernel(own_ref, other_ref, weight_ref, out_ref, rows_ref):
    steps = 3
    heads = weight_ref.shape[0] // HD

    def read(ref):
        tail = ref[:, HD:].astype(f32)
        return ref[:, :HD].astype(f32), tail[:, 0:1] + tail[:, 1:2] + tail[:, 2:3]

    own, own_level = read(own_ref)
    other, other_level = read(other_ref)
    top = jnp.maximum(own_level, other_level)
    own_factor = jnp.exp(own_level - top)
    other_factor = jnp.exp(other_level - top)
    rows_ref[...] = (own * own_factor + other * other_factor) / (own_factor + other_factor)
    attended = jnp.concatenate(
        [rows_ref[h * steps : (h + 1) * steps, :] for h in range(heads)], axis=1
    ).astype(bf16)
    terms = jnp.dot(attended, weight_ref[...], preferred_element_type=f32)
    for k in range(heads):
        rows_ref[k * steps : (k + 1) * steps, :] = terms[:, k * LANES : (k + 1) * LANES]
    out_ref[...] = rows_ref[...].astype(bf16)


def rows_kernel(wide_ref, out_ref):
    steps, width = wide_ref.shape
    for k in range(width // LANES):
        out_ref[k * steps : (k + 1) * steps, :] = wide_ref[:, k * LANES : (k + 1) * LANES].astype(
            f32
        )


def matched(routes_ref, first, count):
    wanted = iota((count, LANES), 0) + first
    return (routes_ref[0:1, :] == wanted) | (routes_ref[1:2, :] == wanted)


def places(routes_ref):
    count = E // 2
    mask = matched(routes_ref, lax.axis_index("ep") * count, 8)
    earlier = (iota((LANES, LANES), 0) < iota((LANES, LANES), 1)).astype(f32).astype(bf16)
    ones = mask.astype(f32)
    place = jnp.dot(ones.astype(bf16), earlier, preferred_element_type=f32).astype(jnp.int32)
    slot = iota((CAP, LANES), 0)
    return [
        jnp.where(place[e : e + 1, :] == slot, ones[e : e + 1, :], 0.0) for e in range(count)
    ]


def hidden_kernel(
    state_ref, gain_ref, router_ref, routes_ref, gate_ref, up_ref, out_ref, wide_ref, scaled_ref, both_ref
):
    groups = state_ref.shape[0] // 72
    steps = 3
    blocks = 24
    tokens = groups * steps
    wide_ref[...] = state_ref[...].astype(f32)
    squares = [jnp.zeros((groups, LANES), f32) for _ in range(steps)]
    for k in range(blocks):
        gain = gain_ref[:, k * LANES : (k + 1) * LANES]
        for s in range(steps):
            block = wide_ref[pl.ds(k * steps + s, groups, stride=72), :]
            squares[s] = squares[s] + block * block
            scaled_ref[s * groups : (s + 1) * groups, k * LANES : (k + 1) * LANES] = (
                block * gain
            ).astype(bf16)
    scaled = scaled_ref[...]
    square = jnp.sum(jnp.concatenate(squares, axis=0), axis=1, keepdims=True)
    diagonal = iota((tokens, LANES), 0) == iota((tokens, LANES), 1)
    square = jnp.sum(jnp.where(diagonal, square, 0.0), axis=0, keepdims=True)
    router = lax.dot_general(
        router_ref[...], scaled, (((1,), (1,)), ((), ())), preferred_element_type=f32
    )
    router = jnp.concatenate([router, jnp.zeros((E, LANES - tokens), f32)], axis=1)
    tables = places(routes_ref)
    width = gate_ref.shape[2]
    both_ref[tokens:, :] = jnp.zeros((LANES - tokens, 2 * width), bf16)
    for e in range(gate_ref.shape[0]):
        both_ref[:tokens, :width] = jnp.dot(
            scaled, gate_ref[e], preferred_element_type=f32
        ).astype(bf16)
        both_ref[:tokens, width:] = jnp.dot(scaled, up_ref[e], preferred_element_type=f32).astype(
            bf16
        )
        out_ref[e * CAP : (e + 1) * CAP, :] = jnp.dot(
            tables[e].astype(bf16), both_ref[...], preferred_element_type=f32
        ).astype(bf16)
    high, middle, _ = pieces(router)
    square_high, square_middle, _ = pieces(square)
    line = iota((8, LANES), 0)
    extra = jnp.concatenate(
        [
            high,
            middle,
            jnp.where(line == 0, square_high, jnp.where(line == 1, square_middle, 0.0)),
            jnp.zeros((8, LANES), f32),
        ],
        axis=1,
    )
    extra = jnp.concatenate([extra, jnp.zeros((8, 4 * LANES), f32)], axis=0)
    out_ref[4 * CAP :, :] = extra.astype(bf16)


def down_kernel(own_ref, other_ref, routes_ref, down_ref, out_ref, mixed_ref, wide_ref):
    groups = out_ref.shape[0] // 72
    steps = 3
    tokens = groups * steps
    width = down_ref.shape[1]
    count = down_ref.shape[0]
    tail = own_ref[4 * CAP :, :].astype(f32) + other_ref[4 * CAP :, :].astype(f32)
    square = tail[0:1, 2 * LANES : 3 * LANES] + tail[1:2, 2 * LANES : 3 * LANES]
    inverse = lax.rsqrt(square / D + epsilon)
    logits = (tail[:E, :LANES] + tail[:E, LANES : 2 * LANES]) * inverse
    every = iota((E, LANES), 0)
    picked = [
        jnp.sum(jnp.where(routes_ref[c : c + 1, :] == every, logits, 0.0), axis=0, keepdims=True)
        for c in range(2)
    ]
    top = jnp.maximum(picked[0], picked[1])
    raised = [jnp.exp(p - top) for p in picked]
    total = raised[0] + raised[1]
    shares = [r / total for r in raised]
    first = lax.axis_index("ep") * count
    tables = places(routes_ref)
    for e in range(count):
        table = tables[e]
        share = jnp.zeros((1, LANES), f32)
        for c in range(2):
            share = share + jnp.where(routes_ref[c : c + 1, :] == first + e, shares[c], 0.0)
        slot_inverse = jnp.sum(table * inverse, axis=1, keepdims=True)
        slot_share = jnp.sum(table * share, axis=1, keepdims=True)
        both = own_ref[e * CAP : (e + 1) * CAP, :].astype(f32) + other_ref[
            e * CAP : (e + 1) * CAP, :
        ].astype(f32)
        both = both * slot_inverse
        gate, up = both[:, :width], both[:, width:]
        activated = (gate / (1.0 + jnp.exp(-gate)) * up).astype(bf16).astype(f32)
        weighted = (activated * slot_share).astype(bf16)
        spread = lax.dot_general(
            table.astype(bf16), weighted, (((0,), (0,)), ((), ())), preferred_element_type=f32
        )
        mixed_ref[:, e * width : (e + 1) * width] = spread[:tokens, :].astype(bf16)
    mixed = mixed_ref[...]
    chunk = 4 * LANES
    for n in range(down_ref.shape[2] // chunk):
        terms = jnp.zeros((tokens, chunk), f32)
        for e in range(count):
            terms = terms + jnp.dot(
                mixed[:, e * width : (e + 1) * width],
                down_ref[e, :, n * chunk : (n + 1) * chunk],
                preferred_element_type=f32,
            )
        for j in range(chunk // LANES):
            k = n * (chunk // LANES) + j
            for s in range(steps):
                wide_ref[pl.ds(k * steps + s, groups, stride=72), :] = terms[
                    s * groups : (s + 1) * groups, j * LANES : (j + 1) * LANES
                ]
    out_ref[...] = wide_ref[...].astype(bf16)


def output_kernel(state_ref, own_ref, other_ref, out_ref, rows_ref):
    steps, width = out_ref.shape
    rows_ref[...] = state_ref[...].astype(f32) + (own_ref[...] + other_ref[...])
    for k in range(width // LANES):
        out_ref[:, k * LANES : (k + 1) * LANES] = rows_ref[k * steps : (k + 1) * steps, :].astype(
            bf16
        )


def on_device(
    queries,
    new_keys,
    new_values,
    cache_keys,
    cache_values,
    lengths,
    residual,
    out_weight,
    norm_gain,
    router_weight,
    routes,
    expert_gate,
    expert_up,
    expert_down,
):
    groups = lax.axis_size("grp")
    steps, _, query_width = queries.shape
    rows = steps * query_width // HD
    struct = jax.ShapeDtypeStruct
    token_count = groups * steps
    routes_row = jnp.pad(
        routes.reshape(token_count, 2).T, ((0, 0), (0, LANES - token_count)), constant_values=-1
    )
    partial = call(
        attention_kernel,
        struct((rows, 2 * HD), bf16),
        (
            lengths,
            queries.reshape(steps, query_width),
            cache_keys[0],
            cache_values[0],
            new_keys[:, 0],
            new_values[:, 0],
        ),
        [SMEM] + [VMEM] * 5,
        [pltpu.VMEM((rows, HD), f32)],
    )
    other = lax.ppermute(partial, "tp", swap)
    terms = call(
        project_kernel,
        struct((rows, LANES), bf16),
        (partial, other, out_weight),
        [VMEM] * 3,
        [pltpu.VMEM((rows, LANES), f32)],
        limit=30,
    )
    residual_rows = call(
        rows_kernel, struct((rows, LANES), f32), (residual[:, 0],), [VMEM]
    )
    other_terms = lax.ppermute(terms, "ep", swap)
    state = (residual_rows + (terms.astype(f32) + other_terms.astype(f32))).astype(bf16)
    all_state = lax.all_to_all(
        jnp.broadcast_to(state[None], (groups, rows, LANES)), "grp", 0, 0
    ).reshape(groups * rows, LANES)
    hidden_rows = 4 * CAP + 16
    width = expert_gate.shape[2]
    hidden = call(
        hidden_kernel,
        struct((hidden_rows, 2 * width), bf16),
        (
            all_state,
            norm_gain.reshape(1, -1),
            router_weight.T,
            routes_row,
            expert_gate,
            expert_up,
        ),
        [VMEM] * 6,
        [
            pltpu.VMEM((groups * rows, LANES), f32),
            pltpu.VMEM((token_count, residual.shape[2]), bf16),
            pltpu.VMEM((LANES, 2 * width), bf16),
        ],
        limit=30,
    )
    other_hidden = lax.ppermute(hidden, "tp", swap)
    sent = call(
        down_kernel,
        struct((groups * rows, LANES), bf16),
        (hidden, other_hidden, routes_row, expert_down),
        [VMEM] * 4,
        [
            pltpu.VMEM((token_count, 4 * width), bf16),
            pltpu.VMEM((groups * rows, LANES), f32),
        ],
        limit=30,
    )
    received = lax.all_to_all(sent.reshape(groups, rows, LANES), "grp", 0, 0)
    summed = jnp.sum(received.astype(f32), axis=0)
    other_summed = lax.ppermute(summed, "ep", swap)
    mixed = call(
        output_kernel,
        struct((steps, residual.shape[2]), bf16),
        (state, summed, other_summed),
        [VMEM] * 3,
        [pltpu.VMEM((rows, LANES), f32)],
    )
    return mixed[:, None]


def solution(mesh):
    in_specs = (
        P(None, "grp", "ep"),
        P(None, "grp", "ep"),
        P(None, "grp", "ep"),
        P("grp", "tp", "ep"),
        P("grp", "tp", "ep"),
        P("grp"),
        P(None, "grp", "tp"),
        P("ep", "tp"),
        P("tp"),
        P("tp", None),
        P(),
        P("ep", "tp", "grp"),
        P("ep", "tp", "grp"),
        P("ep", "grp", "tp"),
    )
    out_specs = P(None, "grp", "tp")
    return jax.shard_map(
        on_device, mesh=mesh, in_specs=in_specs, out_specs=out_specs, check_vma=False
    )
```

```python
import functools

import jax
import jax.numpy as jnp
from jax import lax
from jax.experimental import pallas as pl
from jax.experimental.pallas import tpu as pltpu
from jax.sharding import PartitionSpec as P

D = 6144
HD = 128
E = 8
CAP = 48
PAIRS = 2
STEPS = 3
LANES = 128

far_below = -1e30
epsilon = 1e-05
VMEM = pl.BlockSpec(memory_space=pltpu.VMEM)
SMEM = pl.BlockSpec(memory_space=pltpu.SMEM)
swap = [(0, 1), (1, 0)]
f32 = jnp.float32
bf16 = jnp.bfloat16


def call(kernel, out, operands, specs, scratch=(), limit=4, beside=0):
    return pl.pallas_call(
        kernel,
        out_shape=out,
        in_specs=specs,
        out_specs=jax.tree.map(lambda _: VMEM, out),
        scratch_shapes=scratch,
        compiler_params=pltpu.CompilerParams(vmem_limit_bytes=limit * 2**20),
        cost_estimate=pl.CostEstimate(
            flops=beside * 10**9, bytes_accessed=0, transcendentals=0
        )
        if beside
        else None,
    )(*operands)


def iota(shape, dim):
    return lax.broadcasted_iota(jnp.int32, shape, dim)


def pieces(value):
    high = value.astype(bf16).astype(f32)
    rest = value - high
    middle = rest.astype(bf16).astype(f32)
    return high, middle, rest - middle


def mask_kernel(length_ref, out_ref):
    cached = out_ref.shape[1]
    place = iota(out_ref.shape, 1) + lax.axis_index("tp") * cached
    out_ref[...] = jnp.where(place < length_ref[0], 1.0, 0.0)


def rows_kernel(residual_ref, routes_ref, rows_ref, routes_row_ref, tables_ref, turned_ref):
    steps, width = residual_ref.shape
    groups = routes_ref.shape[2]
    for k in range(width // LANES):
        rows_ref[k * steps : (k + 1) * steps, :] = residual_ref[
            :, k * LANES : (k + 1) * LANES
        ].astype(f32)
    routes_row_ref[...] = jnp.full(routes_row_ref.shape, -1, jnp.int32)
    for s in range(steps):
        routes_row_ref[:, s * groups : (s + 1) * groups] = routes_ref[s]
    count = E // 2
    wanted = iota((E, LANES), 0) + lax.axis_index("ep") * count
    ones = jnp.where(
        (routes_row_ref[0:1, :] == wanted) | (routes_row_ref[1:2, :] == wanted), 1.0, 0.0
    )
    earlier = jnp.where(iota((LANES, LANES), 0) < iota((LANES, LANES), 1), 1.0, 0.0)
    place = jnp.dot(
        ones.astype(bf16), earlier.astype(bf16), preferred_element_type=f32
    ).astype(jnp.int32)
    slot = iota((CAP, LANES), 0)
    for pair in range(PAIRS):
        table = jnp.concatenate(
            [
                jnp.where(place[e : e + 1, :] == slot, ones[e : e + 1, :], 0.0)
                for e in (2 * pair, 2 * pair + 1)
            ]
            + [jnp.zeros((LANES - 2 * CAP, LANES), f32)],
            axis=0,
        )
        tables_ref[pair] = table.astype(bf16)
        turned_ref[pair] = table.T.astype(bf16)


def attention_kernel(
    mask_ref, query_ref, key_ref, value_ref, new_key_ref, new_value_ref, out_ref, rows_ref
):
    steps = query_ref.shape[0]
    heads = query_ref.shape[1] // HD
    kv = key_ref.shape[1] // HD
    rows = heads * steps
    per_kv = rows // kv
    part = lax.axis_index("tp")
    for h in range(heads):
        rows_ref[h * steps : (h + 1) * steps, :] = query_ref[:, h * HD : (h + 1) * HD].astype(f32)
    query = rows_ref[...]
    row = iota((rows, 1), 0)
    owner = [(row >= k * per_kv) & (row < (k + 1) * per_kv) for k in range(kv)]
    step = row % steps
    scale = HD ** (-0.5)
    spread = jnp.concatenate(
        [jnp.where(owner[k], query, 0.0).astype(bf16) for k in range(kv)], axis=1
    )
    scores = (
        lax.dot_general(
            spread, key_ref[...], (((1,), (1,)), ((), ())), preferred_element_type=f32
        )
        * scale
    )
    allowed = mask_ref[0:1, :] > 0.0
    scores = jnp.where(allowed, scores, far_below)
    new_key = new_key_ref[...].astype(f32)

    def chosen(wide, t):
        out = jnp.zeros((rows, HD), f32)
        for k in range(kv):
            out = jnp.where(owner[k], wide[t : t + 1, k * HD : (k + 1) * HD], out)
        return out

    fresh_ok = [(step >= t) & (part == 0) for t in range(steps)]
    fresh = [
        jnp.where(
            fresh_ok[t],
            jnp.sum(query * chosen(new_key, t), axis=1, keepdims=True) * scale,
            far_below,
        )
        for t in range(steps)
    ]
    highest = jnp.max(scores, axis=1, keepdims=True)
    for t in range(steps):
        highest = jnp.maximum(highest, fresh[t])
    exponent = jnp.where(allowed, jnp.exp(scores - highest), 0.0)
    totals = jnp.sum(exponent, axis=1, keepdims=True)
    new_value = new_value_ref[...].astype(f32)
    wide = jnp.dot(exponent.astype(bf16), value_ref[...], preferred_element_type=f32)
    weighted = jnp.zeros((rows, HD), f32)
    for k in range(kv):
        weighted = jnp.where(owner[k], wide[:, k * HD : (k + 1) * HD], weighted)
    for t in range(steps):
        term = jnp.where(fresh_ok[t], jnp.exp(fresh[t] - highest), 0.0)
        totals = totals + term
        weighted = weighted + term.astype(bf16).astype(f32) * chosen(new_value, t)
    present = totals > 0.0
    safe = jnp.where(present, totals, 1.0)
    out_ref[:, :HD] = (weighted / safe).astype(bf16)
    level = jnp.where(present, highest + jnp.log(safe), far_below)
    high, middle, low = pieces(level)
    lane = iota((rows, LANES), 1)
    out_ref[:, HD:] = jnp.where(lane == 0, high, jnp.where(lane == 1, middle, low)).astype(bf16)


def project_kernel(own_ref, other_ref, weight_ref, out_ref, rows_ref):
    steps = 3
    heads = weight_ref.shape[0] // HD

    def read(ref):
        tail = ref[:, HD:].astype(f32)
        return ref[:, :HD].astype(f32), tail[:, 0:1] + tail[:, 1:2] + tail[:, 2:3]

    own, own_level = read(own_ref)
    other, other_level = read(other_ref)
    top = jnp.maximum(own_level, other_level)
    own_factor = jnp.exp(own_level - top)
    other_factor = jnp.exp(other_level - top)
    rows_ref[...] = (own * own_factor + other * other_factor) / (own_factor + other_factor)
    attended = jnp.concatenate(
        [rows_ref[h * steps : (h + 1) * steps, :] for h in range(heads)], axis=1
    ).astype(bf16)
    terms = jnp.dot(attended, weight_ref[...], preferred_element_type=f32)
    for k in range(heads):
        rows_ref[k * steps : (k + 1) * steps, :] = terms[:, k * LANES : (k + 1) * LANES]
    out_ref[...] = rows_ref[...].astype(bf16)


def pack_pair(pair, scaled, tables_ref, gate_ref, up_ref, out_ref, both_ref):
    tokens = scaled.shape[0]
    width = gate_ref.shape[2]
    both_ref[tokens:, :] = jnp.zeros((LANES - tokens, 2 * width), bf16)
    for i in range(2):
        e = 2 * pair + i
        both_ref[:tokens, :width] = jnp.dot(
            scaled, gate_ref[e], preferred_element_type=f32
        ).astype(bf16)
        both_ref[:tokens, width:] = jnp.dot(scaled, up_ref[e], preferred_element_type=f32).astype(
            bf16
        )
        out_ref[i * CAP : (i + 1) * CAP, :] = jnp.dot(
            tables_ref[pair, i * CAP : (i + 1) * CAP, :],
            both_ref[...],
            preferred_element_type=f32,
        ).astype(bf16)


def hidden_kernel(
    state_ref, gain_ref, router_ref, tables_ref, gate_ref, up_ref, out_ref, scaled_ref, wide_ref, both_ref
):
    tokens, width = scaled_ref.shape
    blocks = width // LANES
    stride = STEPS * blocks
    groups = state_ref.shape[0] // stride
    wide_ref[...] = state_ref[...].astype(f32)
    squares = [jnp.zeros((groups, LANES), f32) for _ in range(STEPS)]
    for k in range(blocks):
        gain = gain_ref[:, k * LANES : (k + 1) * LANES]
        for s in range(STEPS):
            block = wide_ref[pl.ds(k * STEPS + s, groups, stride=stride), :]
            squares[s] = squares[s] + block * block
            scaled_ref[s * groups : (s + 1) * groups, k * LANES : (k + 1) * LANES] = (
                block * gain
            ).astype(bf16)
    scaled = scaled_ref[...]
    pack_pair(0, scaled, tables_ref, gate_ref, up_ref, out_ref, both_ref)
    square = jnp.sum(jnp.concatenate(squares, axis=0), axis=1, keepdims=True)
    diagonal = iota((tokens, LANES), 0) == iota((tokens, LANES), 1)
    square = jnp.sum(jnp.where(diagonal, square, 0.0), axis=0, keepdims=True)
    router = lax.dot_general(
        router_ref[...], scaled, (((1,), (1,)), ((), ())), preferred_element_type=f32
    )
    router = jnp.concatenate([router, jnp.zeros((E, LANES - tokens), f32)], axis=1)
    high, middle, _ = pieces(router)
    square_high, square_middle, _ = pieces(square)
    line = iota((E, LANES), 0)
    extra = jnp.concatenate(
        [
            high,
            middle,
            jnp.where(line == 0, square_high, jnp.where(line == 1, square_middle, 0.0)),
            jnp.zeros((E, LANES), f32),
        ],
        axis=1,
    )
    extra = jnp.concatenate([extra, jnp.zeros((8, 4 * LANES), f32)], axis=0)
    out_ref[2 * CAP :, :] = extra.astype(bf16)


def hidden_rest_kernel(scaled_ref, tables_ref, gate_ref, up_ref, out_ref, both_ref):
    pack_pair(1, scaled_ref[...], tables_ref, gate_ref, up_ref, out_ref, both_ref)


def spread_pair(own_ref, other_ref, factors, turned, side_ref, tokens):
    width = side_ref.shape[1] // 2
    side_ref[...] = jnp.zeros(side_ref.shape, bf16)
    both = own_ref[: 2 * CAP, :].astype(f32) + other_ref[: 2 * CAP, :].astype(f32)
    both = both * factors[:, 0:1]
    gate, up = both[:, :width], both[:, width:]
    activated = (gate / (1.0 + jnp.exp(-gate)) * up).astype(bf16).astype(f32)
    weighted = (activated * factors[:, 1:2]).astype(bf16)
    for i in range(2):
        side_ref[i * CAP : (i + 1) * CAP, i * width : (i + 1) * width] = weighted[
            i * CAP : (i + 1) * CAP, :
        ]
    return jnp.dot(turned[:tokens, :], side_ref[...], preferred_element_type=f32).astype(bf16)


def down_kernel(
    own_ref, other_ref, routes_ref, tables_ref, turned_ref, down_ref, terms_ref, factors_ref, side_ref
):
    tokens = terms_ref.shape[0]
    width = down_ref.shape[1]
    tail = own_ref[2 * CAP :, :].astype(f32) + other_ref[2 * CAP :, :].astype(f32)
    square = tail[0:1, 2 * LANES : 3 * LANES] + tail[1:2, 2 * LANES : 3 * LANES]
    inverse = lax.rsqrt(square / D + epsilon)
    logits = (tail[:E, :LANES] + tail[:E, LANES : 2 * LANES]) * inverse
    every = iota((E, LANES), 0)
    picked = [
        jnp.sum(jnp.where(routes_ref[c : c + 1, :] == every, logits, 0.0), axis=0, keepdims=True)
        for c in range(2)
    ]
    top = jnp.maximum(picked[0], picked[1])
    raised = [jnp.exp(p - top) for p in picked]
    total = raised[0] + raised[1]
    shares = [r / total for r in raised]
    first = lax.axis_index("ep") * (2 * PAIRS)

    def factors_of(pair):
        slots = []
        for i in range(2):
            share = jnp.zeros((1, LANES), f32)
            for c in range(2):
                share = share + jnp.where(
                    routes_ref[c : c + 1, :] == first + 2 * pair + i, shares[c], 0.0
                )
            slots.append(jnp.broadcast_to(share, (CAP, LANES)))
        table = tables_ref[pair, : 2 * CAP, :].astype(f32)
        slot_inverse = jnp.sum(table * inverse, axis=1, keepdims=True)
        slot_share = jnp.sum(table * jnp.concatenate(slots, axis=0), axis=1, keepdims=True)
        return jnp.where(iota((2 * CAP, LANES), 1) == 0, slot_inverse, slot_share)

    factors_ref[...] = factors_of(1)
    mixed = spread_pair(own_ref, other_ref, factors_of(0), turned_ref[0], side_ref, tokens)
    terms_ref[...] = sum(
        jnp.dot(
            mixed[:, e * width : (e + 1) * width], down_ref[e], preferred_element_type=f32
        )
        for e in range(2)
    )


def down_rest_kernel(
    own_ref, other_ref, terms_ref, factors_ref, turned_ref, down_ref, out_ref, side_ref, wide_ref
):
    tokens = terms_ref.shape[0]
    width = down_ref.shape[1]
    blocks = down_ref.shape[2] // LANES
    stride = STEPS * blocks
    groups = tokens // STEPS
    mixed = spread_pair(own_ref, other_ref, factors_ref[...], turned_ref[1], side_ref, tokens)
    chunk = 4 * LANES
    for n in range(down_ref.shape[2] // chunk):
        terms = terms_ref[:, n * chunk : (n + 1) * chunk]
        for i in range(2):
            terms = terms + jnp.dot(
                mixed[:, i * width : (i + 1) * width],
                down_ref[2 + i, :, n * chunk : (n + 1) * chunk],
                preferred_element_type=f32,
            )
        for j in range(chunk // LANES):
            k = n * (chunk // LANES) + j
            for s in range(STEPS):
                wide_ref[pl.ds(k * STEPS + s, groups, stride=stride), :] = terms[
                    s * groups : (s + 1) * groups, j * LANES : (j + 1) * LANES
                ]
    out_ref[...] = wide_ref[...].astype(bf16)


def output_kernel(state_ref, own_ref, other_ref, out_ref, rows_ref):
    steps, width = out_ref.shape
    rows_ref[...] = state_ref[...].astype(f32) + (own_ref[...] + other_ref[...])
    for k in range(width // LANES):
        out_ref[:, k * LANES : (k + 1) * LANES] = rows_ref[k * steps : (k + 1) * steps, :].astype(
            bf16
        )


def on_device(
    queries,
    new_keys,
    new_values,
    cache_keys,
    cache_values,
    lengths,
    residual,
    out_weight,
    norm_gain,
    router_weight,
    routes,
    expert_gate,
    expert_up,
    expert_down,
):
    groups = lax.axis_size("grp")
    steps, _, query_width = queries.shape
    rows = steps * query_width // HD
    struct = jax.ShapeDtypeStruct
    token_count = groups * steps
    width = residual.shape[2]
    kv_width = cache_keys.shape[2]
    cached = cache_keys.shape[1]
    mask = call(mask_kernel, struct((8, cached), f32), (lengths,), [SMEM], beside=3)
    partial = call(
        attention_kernel,
        struct((rows, 2 * HD), bf16),
        (
            mask,
            queries.reshape(steps, query_width),
            cache_keys.reshape(cached, kv_width),
            cache_values.reshape(cached, kv_width),
            new_keys.reshape(steps, kv_width),
            new_values.reshape(steps, kv_width),
        ),
        [VMEM] * 6,
        [pltpu.VMEM((rows, HD), f32)],
        beside=7,
    )
    square = struct((PAIRS, LANES, LANES), bf16)
    residual_rows, routes_row, tables, turned = call(
        rows_kernel,
        (struct((rows, LANES), f32), struct((2, LANES), jnp.int32), square, square),
        (residual.reshape(steps, width), routes.transpose(0, 2, 1)),
        [VMEM] * 2,
    )
    other = lax.ppermute(partial, "tp", swap)
    terms = call(
        project_kernel,
        struct((rows, LANES), bf16),
        (partial, other, out_weight),
        [VMEM] * 3,
        [pltpu.VMEM((rows, LANES), f32)],
        beside=20,
    )
    other_terms = lax.ppermute(terms, "ep", swap)
    state = (residual_rows + (terms.astype(f32) + other_terms.astype(f32))).astype(bf16)
    all_state = lax.all_to_all(
        jnp.broadcast_to(state[None], (groups, rows, LANES)), "grp", 0, 0
    ).reshape(groups * rows, LANES)
    hidden_width = 2 * expert_gate.shape[2]
    both = pltpu.VMEM((LANES, hidden_width), bf16)
    hidden, scaled = call(
        hidden_kernel,
        (struct((2 * CAP + 16, hidden_width), bf16), struct((token_count, width), bf16)),
        (
            all_state,
            norm_gain.reshape(1, -1),
            router_weight.T,
            tables,
            expert_gate,
            expert_up,
        ),
        [VMEM] * 6,
        [pltpu.VMEM((groups * rows, LANES), f32), both],
        limit=8,
    )
    other_hidden = lax.ppermute(hidden, "tp", swap)
    hidden_rest = call(
        hidden_rest_kernel,
        struct((2 * CAP, hidden_width), bf16),
        (scaled, tables, expert_gate, expert_up),
        [VMEM] * 4,
        [both],
    )
    other_hidden_rest = lax.ppermute(hidden_rest, "tp", swap)
    side = pltpu.VMEM((LANES, hidden_width), bf16)
    down_terms, factors = call(
        down_kernel,
        (struct((token_count, width), f32), struct((2 * CAP, LANES), f32)),
        (hidden, other_hidden, routes_row, tables, turned, expert_down),
        [VMEM] * 6,
        [side],
        limit=8,
    )
    sent = call(
        down_rest_kernel,
        struct((groups * rows, LANES), bf16),
        (hidden_rest, other_hidden_rest, down_terms, factors, turned, expert_down),
        [VMEM] * 6,
        [side, pltpu.VMEM((groups * rows, LANES), f32)],
        limit=8,
    )
    received = lax.all_to_all(sent.reshape(groups, rows, LANES), "grp", 0, 0)
    summed = jnp.sum(received.astype(f32), axis=0)
    other_summed = lax.ppermute(summed, "ep", swap)
    mixed = call(
        output_kernel,
        struct((steps, width), bf16),
        (state, summed, other_summed),
        [VMEM] * 3,
        [pltpu.VMEM((rows, LANES), f32)],
    )
    return mixed[:, None]


def solution(mesh):
    in_specs = (
        P(None, "grp", "ep"),
        P(None, "grp", "ep"),
        P(None, "grp", "ep"),
        P("grp", "tp", "ep"),
        P("grp", "tp", "ep"),
        P("grp"),
        P(None, "grp", "tp"),
        P("ep", "tp"),
        P("tp"),
        P("tp", None),
        P(),
        P("ep", "tp", "grp"),
        P("ep", "tp", "grp"),
        P("ep", "grp", "tp"),
    )
    out_specs = P(None, "grp", "tp")
    return jax.shard_map(
        on_device, mesh=mesh, in_specs=in_specs, out_specs=out_specs, check_vma=False
    )
```

```python
import functools

import jax
import jax.numpy as jnp
from jax import lax
from jax.experimental import pallas as pl
from jax.experimental.pallas import tpu as pltpu
from jax.sharding import PartitionSpec as P

D = 6144
HD = 128
E = 8
CAP = 48
PAIRS = 2
STEPS = 3
PARTS = 4
LANES = 128

far_below = -1e30
epsilon = 1e-05
VMEM = pl.BlockSpec(memory_space=pltpu.VMEM)
SMEM = pl.BlockSpec(memory_space=pltpu.SMEM)
swap = [(0, 1), (1, 0)]
f32 = jnp.float32
bf16 = jnp.bfloat16


def call(kernel, out, operands, specs, scratch=(), limit=4, beside=0):
    return pl.pallas_call(
        kernel,
        out_shape=out,
        in_specs=specs,
        out_specs=jax.tree.map(lambda _: VMEM, out),
        scratch_shapes=scratch,
        compiler_params=pltpu.CompilerParams(vmem_limit_bytes=limit * 2**20),
        cost_estimate=pl.CostEstimate(
            flops=beside * 10**9, bytes_accessed=0, transcendentals=0
        )
        if beside
        else None,
    )(*operands)


def iota(shape, dim):
    return lax.broadcasted_iota(jnp.int32, shape, dim)


def pieces(value):
    high = value.astype(bf16).astype(f32)
    rest = value - high
    middle = rest.astype(bf16).astype(f32)
    return high, middle, rest - middle


def mask_kernel(length_ref, out_ref):
    cached = out_ref.shape[1]
    place = iota(out_ref.shape, 1) + lax.axis_index("tp") * cached
    out_ref[...] = jnp.where(place < length_ref[0], 1.0, 0.0)


def rows_kernel(residual_ref, routes_ref, rows_ref, routes_row_ref, tables_ref, turned_ref):
    steps, width = residual_ref.shape
    groups = routes_ref.shape[2]
    for k in range(width // LANES):
        rows_ref[k * steps : (k + 1) * steps, :] = residual_ref[
            :, k * LANES : (k + 1) * LANES
        ].astype(f32)
    routes_row_ref[...] = jnp.full(routes_row_ref.shape, -1, jnp.int32)
    for s in range(steps):
        routes_row_ref[:, s * groups : (s + 1) * groups] = routes_ref[s]
    count = E // 2
    wanted = iota((E, LANES), 0) + lax.axis_index("ep") * count
    ones = jnp.where(
        (routes_row_ref[0:1, :] == wanted) | (routes_row_ref[1:2, :] == wanted), 1.0, 0.0
    )
    earlier = jnp.where(iota((LANES, LANES), 0) < iota((LANES, LANES), 1), 1.0, 0.0)
    place = jnp.dot(
        ones.astype(bf16), earlier.astype(bf16), preferred_element_type=f32
    ).astype(jnp.int32)
    slot = iota((CAP, LANES), 0)
    for pair in range(PAIRS):
        table = jnp.concatenate(
            [
                jnp.where(place[e : e + 1, :] == slot, ones[e : e + 1, :], 0.0)
                for e in (2 * pair, 2 * pair + 1)
            ]
            + [jnp.zeros((LANES - 2 * CAP, LANES), f32)],
            axis=0,
        )
        tables_ref[pair] = table.astype(bf16)
        turned_ref[pair] = table.T.astype(bf16)


def attention_kernel(
    mask_ref, query_ref, key_ref, value_ref, new_key_ref, new_value_ref, out_ref, rows_ref
):
    steps = query_ref.shape[0]
    heads = query_ref.shape[1] // HD
    kv = key_ref.shape[1] // HD
    rows = heads * steps
    per_kv = rows // kv
    part = lax.axis_index("tp")
    for h in range(heads):
        rows_ref[h * steps : (h + 1) * steps, :] = query_ref[:, h * HD : (h + 1) * HD].astype(f32)
    query = rows_ref[...]
    row = iota((rows, 1), 0)
    owner = [(row >= k * per_kv) & (row < (k + 1) * per_kv) for k in range(kv)]
    step = row % steps
    scale = HD ** (-0.5)
    spread = jnp.concatenate(
        [jnp.where(owner[k], query, 0.0).astype(bf16) for k in range(kv)], axis=1
    )
    scores = (
        lax.dot_general(
            spread, key_ref[...], (((1,), (1,)), ((), ())), preferred_element_type=f32
        )
        * scale
    )
    allowed = mask_ref[0:1, :] > 0.0
    scores = jnp.where(allowed, scores, far_below)
    new_key = new_key_ref[...].astype(f32)

    def chosen(wide, t):
        out = jnp.zeros((rows, HD), f32)
        for k in range(kv):
            out = jnp.where(owner[k], wide[t : t + 1, k * HD : (k + 1) * HD], out)
        return out

    fresh_ok = [(step >= t) & (part == 0) for t in range(steps)]
    fresh = [
        jnp.where(
            fresh_ok[t],
            jnp.sum(query * chosen(new_key, t), axis=1, keepdims=True) * scale,
            far_below,
        )
        for t in range(steps)
    ]
    highest = jnp.max(scores, axis=1, keepdims=True)
    for t in range(steps):
        highest = jnp.maximum(highest, fresh[t])
    exponent = jnp.where(allowed, jnp.exp(scores - highest), 0.0)
    totals = jnp.sum(exponent, axis=1, keepdims=True)
    new_value = new_value_ref[...].astype(f32)
    wide = jnp.dot(exponent.astype(bf16), value_ref[...], preferred_element_type=f32)
    weighted = jnp.zeros((rows, HD), f32)
    for k in range(kv):
        weighted = jnp.where(owner[k], wide[:, k * HD : (k + 1) * HD], weighted)
    for t in range(steps):
        term = jnp.where(fresh_ok[t], jnp.exp(fresh[t] - highest), 0.0)
        totals = totals + term
        weighted = weighted + term.astype(bf16).astype(f32) * chosen(new_value, t)
    present = totals > 0.0
    safe = jnp.where(present, totals, 1.0)
    out_ref[:, :HD] = (weighted / safe).astype(bf16)
    level = jnp.where(present, highest + jnp.log(safe), far_below)
    high, middle, low = pieces(level)
    lane = iota((rows, LANES), 1)
    out_ref[:, HD:] = jnp.where(lane == 0, high, jnp.where(lane == 1, middle, low)).astype(bf16)


def join_kernel(own_ref, other_ref, attended_ref, rows_ref):
    steps = attended_ref.shape[0]
    heads = own_ref.shape[0] // steps

    def read(ref):
        tail = ref[:, HD:].astype(f32)
        return ref[:, :HD].astype(f32), tail[:, 0:1] + tail[:, 1:2] + tail[:, 2:3]

    own, own_level = read(own_ref)
    other, other_level = read(other_ref)
    top = jnp.maximum(own_level, other_level)
    own_factor = jnp.exp(own_level - top)
    other_factor = jnp.exp(other_level - top)
    rows_ref[...] = (own * own_factor + other * other_factor) / (own_factor + other_factor)
    attended_ref[...] = jnp.concatenate(
        [rows_ref[h * steps : (h + 1) * steps, :] for h in range(heads)], axis=1
    ).astype(bf16)


def project_kernel(attended_ref, weight_ref, out_ref, rows_ref):
    steps = attended_ref.shape[0]
    terms = jnp.dot(attended_ref[...], weight_ref[...], preferred_element_type=f32)
    for k in range(weight_ref.shape[1] // LANES):
        rows_ref[k * steps : (k + 1) * steps, :] = terms[:, k * LANES : (k + 1) * LANES]
    out_ref[...] = rows_ref[...].astype(bf16)


def pack_pair(pair, scaled_refs, tables_ref, gate_ref, up_ref, out_ref, sums_ref, both_ref):
    tokens, part = scaled_refs[0].shape
    width = gate_ref.shape[2]
    both_ref[:, tokens:, :] = jnp.zeros((2, LANES - tokens, 2 * width), bf16)
    last = len(scaled_refs) - 1
    for n, scaled_ref in enumerate(scaled_refs):
        scaled = scaled_ref[...]
        for i in range(2):
            for j, weight_ref in enumerate((gate_ref, up_ref)):
                terms = jnp.dot(
                    scaled,
                    weight_ref[2 * pair + i, n * part : (n + 1) * part, :],
                    preferred_element_type=f32,
                )
                if n > 0:
                    terms = terms + sums_ref[2 * i + j]
                if n < last:
                    sums_ref[2 * i + j] = terms
                else:
                    both_ref[i, :tokens, j * width : (j + 1) * width] = terms.astype(bf16)
    for i in range(2):
        out_ref[i * CAP : (i + 1) * CAP, :] = jnp.dot(
            tables_ref[pair, i * CAP : (i + 1) * CAP, :],
            both_ref[i],
            preferred_element_type=f32,
        ).astype(bf16)


def hidden_kernel(
    state_ref, gain_ref, router_ref, tables_ref, gate_ref, up_ref, out_ref, *refs
):
    *scaled_refs, wide_ref, sums_ref, both_ref = refs
    tokens, part = scaled_refs[0].shape
    blocks = len(scaled_refs) * part // LANES
    stride = STEPS * blocks
    groups = state_ref.shape[0] // stride
    wide_ref[...] = state_ref[...].astype(f32)
    squares = [jnp.zeros((groups, LANES), f32) for _ in range(STEPS)]
    for k in range(blocks):
        gain = gain_ref[:, k * LANES : (k + 1) * LANES]
        scaled_ref = scaled_refs[k * LANES // part]
        column = k * LANES % part
        for s in range(STEPS):
            block = wide_ref[pl.ds(k * STEPS + s, groups, stride=stride), :]
            squares[s] = squares[s] + block * block
            scaled_ref[s * groups : (s + 1) * groups, column : column + LANES] = (
                block * gain
            ).astype(bf16)
    pack_pair(0, scaled_refs, tables_ref, gate_ref, up_ref, out_ref, sums_ref, both_ref)
    square = jnp.sum(jnp.concatenate(squares, axis=0), axis=1, keepdims=True)
    diagonal = iota((tokens, LANES), 0) == iota((tokens, LANES), 1)
    square = jnp.sum(jnp.where(diagonal, square, 0.0), axis=0, keepdims=True)
    router = sum(
        lax.dot_general(
            router_ref[:, n * part : (n + 1) * part],
            ref[...],
            (((1,), (1,)), ((), ())),
            preferred_element_type=f32,
        )
        for n, ref in enumerate(scaled_refs)
    )
    router = jnp.concatenate([router, jnp.zeros((E, LANES - tokens), f32)], axis=1)
    high, middle, _ = pieces(router)
    square_high, square_middle, _ = pieces(square)
    line = iota((E, LANES), 0)
    extra = jnp.concatenate(
        [
            high,
            middle,
            jnp.where(line == 0, square_high, jnp.where(line == 1, square_middle, 0.0)),
            jnp.zeros((E, LANES), f32),
        ],
        axis=1,
    )
    out_ref[2 * CAP :, :] = extra.astype(bf16)


def hidden_rest_kernel(*refs):
    *scaled_refs, tables_ref, gate_ref, up_ref, out_ref, sums_ref, both_ref = refs
    pack_pair(1, scaled_refs, tables_ref, gate_ref, up_ref, out_ref, sums_ref, both_ref)


def spread_pair(own_ref, other_ref, factors, turned, side_ref, tokens):
    width = side_ref.shape[1] // 2
    side_ref[...] = jnp.zeros(side_ref.shape, bf16)
    both = own_ref[: 2 * CAP, :].astype(f32) + other_ref[: 2 * CAP, :].astype(f32)
    both = both * factors[:, 0:1]
    gate, up = both[:, :width], both[:, width:]
    activated = (gate / (1.0 + jnp.exp(-gate)) * up).astype(bf16).astype(f32)
    weighted = (activated * factors[:, 1:2]).astype(bf16)
    for i in range(2):
        side_ref[i * CAP : (i + 1) * CAP, i * width : (i + 1) * width] = weighted[
            i * CAP : (i + 1) * CAP, :
        ]
    return jnp.dot(turned[:tokens, :], side_ref[...], preferred_element_type=f32).astype(bf16)


def down_kernel(
    own_ref, other_ref, routes_ref, tables_ref, turned_ref, down_ref, terms_ref, factors_ref, side_ref
):
    tokens = terms_ref.shape[0]
    width = down_ref.shape[1]
    tail = own_ref[2 * CAP :, :].astype(f32) + other_ref[2 * CAP :, :].astype(f32)
    square = tail[0:1, 2 * LANES : 3 * LANES] + tail[1:2, 2 * LANES : 3 * LANES]
    inverse = lax.rsqrt(square / D + epsilon)
    logits = (tail[:E, :LANES] + tail[:E, LANES : 2 * LANES]) * inverse
    every = iota((E, LANES), 0)
    picked = [
        jnp.sum(jnp.where(routes_ref[c : c + 1, :] == every, logits, 0.0), axis=0, keepdims=True)
        for c in range(2)
    ]
    top = jnp.maximum(picked[0], picked[1])
    raised = [jnp.exp(p - top) for p in picked]
    total = raised[0] + raised[1]
    shares = [r / total for r in raised]
    first = lax.axis_index("ep") * (2 * PAIRS)

    def factors_of(pair):
        slots = []
        for i in range(2):
            share = jnp.zeros((1, LANES), f32)
            for c in range(2):
                share = share + jnp.where(
                    routes_ref[c : c + 1, :] == first + 2 * pair + i, shares[c], 0.0
                )
            slots.append(jnp.broadcast_to(share, (CAP, LANES)))
        table = tables_ref[pair, : 2 * CAP, :].astype(f32)
        slot_inverse = jnp.sum(table * inverse, axis=1, keepdims=True)
        slot_share = jnp.sum(table * jnp.concatenate(slots, axis=0), axis=1, keepdims=True)
        return jnp.where(iota((2 * CAP, LANES), 1) == 0, slot_inverse, slot_share)

    factors_ref[...] = factors_of(1)
    mixed = spread_pair(own_ref, other_ref, factors_of(0), turned_ref[0], side_ref, tokens)
    terms_ref[...] = sum(
        jnp.dot(
            mixed[:, e * width : (e + 1) * width], down_ref[e], preferred_element_type=f32
        )
        for e in range(2)
    )


def down_rest_kernel(
    own_ref, other_ref, terms_ref, factors_ref, turned_ref, down_ref, out_ref, side_ref, wide_ref
):
    tokens = terms_ref.shape[0]
    width = down_ref.shape[1]
    blocks = down_ref.shape[2] // LANES
    stride = STEPS * blocks
    groups = tokens // STEPS
    mixed = spread_pair(own_ref, other_ref, factors_ref[...], turned_ref[1], side_ref, tokens)
    chunk = 4 * LANES
    for n in range(down_ref.shape[2] // chunk):
        terms = terms_ref[:, n * chunk : (n + 1) * chunk]
        for i in range(2):
            terms = terms + jnp.dot(
                mixed[:, i * width : (i + 1) * width],
                down_ref[2 + i, :, n * chunk : (n + 1) * chunk],
                preferred_element_type=f32,
            )
        for j in range(chunk // LANES):
            k = n * (chunk // LANES) + j
            for s in range(STEPS):
                wide_ref[pl.ds(k * STEPS + s, groups, stride=stride), :] = terms[
                    s * groups : (s + 1) * groups, j * LANES : (j + 1) * LANES
                ]
    out_ref[...] = wide_ref[...].astype(bf16)


def output_kernel(state_ref, own_ref, other_ref, out_ref, rows_ref):
    steps, width = out_ref.shape
    rows_ref[...] = state_ref[...].astype(f32) + (own_ref[...] + other_ref[...])
    for k in range(width // LANES):
        out_ref[:, k * LANES : (k + 1) * LANES] = rows_ref[k * steps : (k + 1) * steps, :].astype(
            bf16
        )


def on_device(
    queries,
    new_keys,
    new_values,
    cache_keys,
    cache_values,
    lengths,
    residual,
    out_weight,
    norm_gain,
    router_weight,
    routes,
    expert_gate,
    expert_up,
    expert_down,
):
    groups = lax.axis_size("grp")
    steps, _, query_width = queries.shape
    rows = steps * query_width // HD
    struct = jax.ShapeDtypeStruct
    token_count = groups * steps
    width = residual.shape[2]
    kv_width = cache_keys.shape[2]
    cached = cache_keys.shape[1]
    mask = call(mask_kernel, struct((8, cached), f32), (lengths,), [SMEM], beside=3)
    partial = call(
        attention_kernel,
        struct((rows, 2 * HD), bf16),
        (
            mask,
            queries.reshape(steps, query_width),
            cache_keys.reshape(cached, kv_width),
            cache_values.reshape(cached, kv_width),
            new_keys.reshape(steps, kv_width),
            new_values.reshape(steps, kv_width),
        ),
        [VMEM] * 6,
        [pltpu.VMEM((rows, HD), f32)],
        beside=2,
    )
    square = struct((PAIRS, LANES, LANES), bf16)
    residual_rows, routes_row, tables, turned = call(
        rows_kernel,
        (struct((rows, LANES), f32), struct((2, LANES), jnp.int32), square, square),
        (residual.reshape(steps, width), routes.transpose(0, 2, 1)),
        [VMEM] * 2,
    )
    other = lax.ppermute(partial, "tp", swap)
    attended = call(
        join_kernel,
        struct((steps, query_width), bf16),
        (partial, other),
        [VMEM] * 2,
        [pltpu.VMEM((rows, HD), f32)],
        beside=2,
    )
    terms = call(
        project_kernel,
        struct((rows, LANES), bf16),
        (attended, out_weight),
        [VMEM] * 2,
        [pltpu.VMEM((rows, LANES), f32)],
        beside=20,
    )
    other_terms = lax.ppermute(terms, "ep", swap)
    state = (residual_rows + (terms.astype(f32) + other_terms.astype(f32))).astype(bf16)
    all_state = lax.all_to_all(
        jnp.broadcast_to(state[None], (groups, rows, LANES)), "grp", 0, 0
    ).reshape(groups * rows, LANES)
    hidden_width = 2 * expert_gate.shape[2]
    both = pltpu.VMEM((2, LANES, hidden_width), bf16)
    sums = pltpu.VMEM((4, token_count, hidden_width // 2), f32)
    hidden, *scaled = call(
        hidden_kernel,
        (
            struct((2 * CAP + E, hidden_width), bf16),
            *[struct((token_count, width // PARTS), bf16)] * PARTS,
        ),
        (
            all_state,
            norm_gain.reshape(1, -1),
            router_weight.T,
            tables,
            expert_gate,
            expert_up,
        ),
        [VMEM] * 6,
        [pltpu.VMEM((groups * rows, LANES), f32), sums, both],
        limit=8,
    )
    other_hidden = lax.ppermute(hidden, "tp", swap)
    hidden_rest = call(
        hidden_rest_kernel,
        struct((2 * CAP, hidden_width), bf16),
        (*scaled, tables, expert_gate, expert_up),
        [VMEM] * (PARTS + 3),
        [sums, both],
    )
    other_hidden_rest = lax.ppermute(hidden_rest, "tp", swap)
    side = pltpu.VMEM((LANES, hidden_width), bf16)
    down_terms, factors = call(
        down_kernel,
        (struct((token_count, width), f32), struct((2 * CAP, LANES), f32)),
        (hidden, other_hidden, routes_row, tables, turned, expert_down),
        [VMEM] * 6,
        [side],
        limit=8,
    )
    sent = call(
        down_rest_kernel,
        struct((groups * rows, LANES), bf16),
        (hidden_rest, other_hidden_rest, down_terms, factors, turned, expert_down),
        [VMEM] * 6,
        [side, pltpu.VMEM((groups * rows, LANES), f32)],
        limit=8,
    )
    received = lax.all_to_all(sent.reshape(groups, rows, LANES), "grp", 0, 0)
    summed = jnp.sum(received.astype(f32), axis=0)
    other_summed = lax.ppermute(summed, "ep", swap)
    mixed = call(
        output_kernel,
        struct((steps, width), bf16),
        (state, summed, other_summed),
        [VMEM] * 3,
        [pltpu.VMEM((rows, LANES), f32)],
    )
    return mixed[:, None]


def solution(mesh):
    in_specs = (
        P(None, "grp", "ep"),
        P(None, "grp", "ep"),
        P(None, "grp", "ep"),
        P("grp", "tp", "ep"),
        P("grp", "tp", "ep"),
        P("grp"),
        P(None, "grp", "tp"),
        P("ep", "tp"),
        P("tp"),
        P("tp", None),
        P(),
        P("ep", "tp", "grp"),
        P("ep", "tp", "grp"),
        P("ep", "grp", "tp"),
    )
    out_specs = P(None, "grp", "tp")
    return jax.shard_map(
        on_device, mesh=mesh, in_specs=in_specs, out_specs=out_specs, check_vma=False
    )
```

```python
import functools

import jax
import jax.numpy as jnp
from jax import lax
from jax.experimental import pallas as pl
from jax.experimental.pallas import tpu as pltpu
from jax.sharding import PartitionSpec as P

D = 6144
HD = 128
E = 8
CAP = 48
PAIRS = 2
STEPS = 3
PARTS = 4
EXTRA = 16
LANES = 128

far_below = -1e30
epsilon = 1e-05
VMEM = pl.BlockSpec(memory_space=pltpu.VMEM)
SMEM = pl.BlockSpec(memory_space=pltpu.SMEM)
swap = [(0, 1), (1, 0)]
f32 = jnp.float32
bf16 = jnp.bfloat16


def call(kernel, out, operands, specs, scratch=(), limit=4, beside=0):
    return pl.pallas_call(
        kernel,
        out_shape=out,
        in_specs=specs,
        out_specs=jax.tree.map(lambda _: VMEM, out),
        scratch_shapes=scratch,
        compiler_params=pltpu.CompilerParams(vmem_limit_bytes=limit * 2**20),
        cost_estimate=pl.CostEstimate(
            flops=beside * 10**9, bytes_accessed=0, transcendentals=0
        )
        if beside
        else None,
    )(*operands)


def iota(shape, dim):
    return lax.broadcasted_iota(jnp.int32, shape, dim)


def pieces(value):
    high = value.astype(bf16).astype(f32)
    rest = value - high
    middle = rest.astype(bf16).astype(f32)
    return high, middle, rest - middle


def mask_kernel(length_ref, out_ref):
    cached = out_ref.shape[1]
    place = iota(out_ref.shape, 1) + lax.axis_index("tp") * cached
    out_ref[...] = jnp.where(place < length_ref[0], 1.0, 0.0)


def rows_kernel(residual_ref, routes_ref, rows_ref, routes_row_ref, tables_ref, turned_ref):
    steps, width = residual_ref.shape
    groups = routes_ref.shape[2]
    for k in range(width // LANES):
        rows_ref[k * steps : (k + 1) * steps, :] = residual_ref[
            :, k * LANES : (k + 1) * LANES
        ].astype(f32)
    routes_row_ref[...] = jnp.full(routes_row_ref.shape, -1, jnp.int32)
    for s in range(steps):
        routes_row_ref[:, s * groups : (s + 1) * groups] = routes_ref[s]
    count = E // 2
    wanted = iota((E, LANES), 0) + lax.axis_index("ep") * count
    ones = jnp.where(
        (routes_row_ref[0:1, :] == wanted) | (routes_row_ref[1:2, :] == wanted), 1.0, 0.0
    )
    earlier = jnp.where(iota((LANES, LANES), 0) < iota((LANES, LANES), 1), 1.0, 0.0)
    place = jnp.dot(
        ones.astype(bf16), earlier.astype(bf16), preferred_element_type=f32
    ).astype(jnp.int32)
    slot = iota((CAP, LANES), 0)
    for pair in range(PAIRS):
        table = jnp.concatenate(
            [
                jnp.where(place[e : e + 1, :] == slot, ones[e : e + 1, :], 0.0)
                for e in (2 * pair, 2 * pair + 1)
            ]
            + [jnp.zeros((LANES - 2 * CAP, LANES), f32)],
            axis=0,
        )
        tables_ref[pair] = table.astype(bf16)
        turned_ref[pair] = table.T.astype(bf16)


def attention_kernel(
    mask_ref, query_ref, key_ref, value_ref, new_key_ref, new_value_ref, out_ref, rows_ref
):
    steps = query_ref.shape[0]
    heads = query_ref.shape[1] // HD
    kv = key_ref.shape[1] // HD
    rows = heads * steps
    per_kv = rows // kv
    part = lax.axis_index("tp")
    for h in range(heads):
        rows_ref[h * steps : (h + 1) * steps, :] = query_ref[:, h * HD : (h + 1) * HD].astype(f32)
    query = rows_ref[...]
    row = iota((rows, 1), 0)
    owner = [(row >= k * per_kv) & (row < (k + 1) * per_kv) for k in range(kv)]
    step = row % steps
    scale = HD ** (-0.5)
    spread = jnp.concatenate(
        [jnp.where(owner[k], query, 0.0).astype(bf16) for k in range(kv)], axis=1
    )
    scores = (
        lax.dot_general(
            spread, key_ref[...], (((1,), (1,)), ((), ())), preferred_element_type=f32
        )
        * scale
    )
    allowed = mask_ref[0:1, :] > 0.0
    scores = jnp.where(allowed, scores, far_below)
    new_key = new_key_ref[...].astype(f32)

    def chosen(wide, t):
        out = jnp.zeros((rows, HD), f32)
        for k in range(kv):
            out = jnp.where(owner[k], wide[t : t + 1, k * HD : (k + 1) * HD], out)
        return out

    fresh_ok = [(step >= t) & (part == 0) for t in range(steps)]
    fresh = [
        jnp.where(
            fresh_ok[t],
            jnp.sum(query * chosen(new_key, t), axis=1, keepdims=True) * scale,
            far_below,
        )
        for t in range(steps)
    ]
    highest = jnp.max(scores, axis=1, keepdims=True)
    for t in range(steps):
        highest = jnp.maximum(highest, fresh[t])
    exponent = jnp.where(allowed, jnp.exp(scores - highest), 0.0)
    totals = jnp.sum(exponent, axis=1, keepdims=True)
    new_value = new_value_ref[...].astype(f32)
    wide = jnp.dot(exponent.astype(bf16), value_ref[...], preferred_element_type=f32)
    weighted = jnp.zeros((rows, HD), f32)
    for k in range(kv):
        weighted = jnp.where(owner[k], wide[:, k * HD : (k + 1) * HD], weighted)
    for t in range(steps):
        term = jnp.where(fresh_ok[t], jnp.exp(fresh[t] - highest), 0.0)
        totals = totals + term
        weighted = weighted + term.astype(bf16).astype(f32) * chosen(new_value, t)
    present = totals > 0.0
    safe = jnp.where(present, totals, 1.0)
    out_ref[:, :HD] = (weighted / safe).astype(bf16)
    tail = pieces(highest) + pieces(totals)
    lane = iota((rows, LANES), 1)
    row_tail = jnp.zeros((rows, LANES), f32)
    for i, piece in enumerate(tail):
        row_tail = jnp.where(lane == i, piece, row_tail)
    out_ref[:, HD:] = row_tail.astype(bf16)


def join_kernel(own_ref, other_ref, attended_ref, rows_ref):
    steps = attended_ref.shape[0]
    heads = own_ref.shape[0] // steps

    def read(ref):
        tail = ref[:, HD:].astype(f32)
        highest = tail[:, 0:1] + tail[:, 1:2] + tail[:, 2:3]
        totals = tail[:, 3:4] + tail[:, 4:5] + tail[:, 5:6]
        return ref[:, :HD].astype(f32), highest, totals

    own, own_highest, own_totals = read(own_ref)
    other, other_highest, other_totals = read(other_ref)
    top = jnp.maximum(own_highest, other_highest)
    own_factor = own_totals * jnp.exp(own_highest - top)
    other_factor = other_totals * jnp.exp(other_highest - top)
    rows_ref[...] = (own * own_factor + other * other_factor) / (own_factor + other_factor)
    attended_ref[...] = jnp.concatenate(
        [rows_ref[h * steps : (h + 1) * steps, :] for h in range(heads)], axis=1
    ).astype(bf16)


def project_kernel(attended_ref, weight_ref, out_ref, rows_ref):
    steps = attended_ref.shape[0]
    terms = jnp.dot(attended_ref[...], weight_ref[...], preferred_element_type=f32)
    for k in range(weight_ref.shape[1] // LANES):
        rows_ref[k * steps : (k + 1) * steps, :] = terms[:, k * LANES : (k + 1) * LANES]
    out_ref[...] = rows_ref[...].astype(bf16)


def pack_pair(pair, scaled_refs, tables_ref, gate_ref, up_ref, out_ref, sums_ref, both_ref):
    tokens, part = scaled_refs[0].shape
    width = gate_ref.shape[2]
    both_ref[:, tokens:, :] = jnp.zeros((2, LANES - tokens, 2 * width), bf16)
    last = len(scaled_refs) - 1
    for n, scaled_ref in enumerate(scaled_refs):
        scaled = scaled_ref[...]
        for i in range(2):
            for j, weight_ref in enumerate((gate_ref, up_ref)):
                terms = jnp.dot(
                    scaled,
                    weight_ref[2 * pair + i, n * part : (n + 1) * part, :],
                    preferred_element_type=f32,
                )
                if n > 0:
                    terms = terms + sums_ref[2 * i + j]
                if n < last:
                    sums_ref[2 * i + j] = terms
                else:
                    both_ref[i, :tokens, j * width : (j + 1) * width] = terms.astype(bf16)
    for i in range(2):
        out_ref[i * CAP : (i + 1) * CAP, :] = jnp.dot(
            tables_ref[pair, i * CAP : (i + 1) * CAP, :],
            both_ref[i],
            preferred_element_type=f32,
        ).astype(bf16)


def hidden_kernel(
    state_ref, gain_ref, router_ref, tables_ref, gate_ref, up_ref, out_ref, *refs
):
    *scaled_refs, wide_ref, sums_ref, both_ref = refs
    tokens, part = scaled_refs[0].shape
    blocks = len(scaled_refs) * part // LANES
    stride = STEPS * blocks
    groups = state_ref.shape[0] // stride
    wide_ref[...] = state_ref[...].astype(f32)
    squares = [jnp.zeros((groups, LANES), f32) for _ in range(STEPS)]
    for k in range(blocks):
        gain = gain_ref[:, k * LANES : (k + 1) * LANES]
        scaled_ref = scaled_refs[k * LANES // part]
        column = k * LANES % part
        for s in range(STEPS):
            block = wide_ref[pl.ds(k * STEPS + s, groups, stride=stride), :]
            squares[s] = squares[s] + block * block
            scaled_ref[s * groups : (s + 1) * groups, column : column + LANES] = (
                block * gain
            ).astype(bf16)
    pack_pair(0, scaled_refs, tables_ref, gate_ref, up_ref, out_ref, sums_ref, both_ref)
    square = jnp.sum(jnp.concatenate(squares, axis=0), axis=1, keepdims=True)
    diagonal = iota((tokens, LANES), 0) == iota((tokens, LANES), 1)
    square = jnp.sum(jnp.where(diagonal, square, 0.0), axis=0, keepdims=True)
    router = sum(
        lax.dot_general(
            router_ref[:, n * part : (n + 1) * part],
            ref[...],
            (((1,), (1,)), ((), ())),
            preferred_element_type=f32,
        )
        for n, ref in enumerate(scaled_refs)
    )
    router = jnp.concatenate([router, jnp.zeros((E, LANES - tokens), f32)], axis=1)
    high, middle, _ = pieces(router)
    square_high, square_middle, _ = pieces(square)
    line = iota((E, LANES), 0)
    extra = jnp.concatenate(
        [
            high,
            middle,
            jnp.where(line == 0, square_high, jnp.where(line == 1, square_middle, 0.0)),
            jnp.zeros((E, LANES), f32),
        ],
        axis=1,
    )
    extra = jnp.concatenate([extra, jnp.zeros((EXTRA - E, 4 * LANES), f32)], axis=0)
    out_ref[2 * CAP :, :] = extra.astype(bf16)


def hidden_rest_kernel(*refs):
    *scaled_refs, tables_ref, gate_ref, up_ref, out_ref, sums_ref, both_ref = refs
    pack_pair(1, scaled_refs, tables_ref, gate_ref, up_ref, out_ref, sums_ref, both_ref)


def spread_pair(own_ref, other_ref, factors, turned, side_ref, tokens):
    width = side_ref.shape[1] // 2
    side_ref[...] = jnp.zeros(side_ref.shape, bf16)
    both = own_ref[: 2 * CAP, :].astype(f32) + other_ref[: 2 * CAP, :].astype(f32)
    both = both * factors[:, 0:1]
    gate, up = both[:, :width], both[:, width:]
    activated = (gate / (1.0 + jnp.exp(-gate)) * up).astype(bf16).astype(f32)
    weighted = (activated * factors[:, 1:2]).astype(bf16)
    for i in range(2):
        side_ref[i * CAP : (i + 1) * CAP, i * width : (i + 1) * width] = weighted[
            i * CAP : (i + 1) * CAP, :
        ]
    return jnp.dot(turned[:tokens, :], side_ref[...], preferred_element_type=f32).astype(bf16)


def down_kernel(
    own_ref, other_ref, routes_ref, tables_ref, turned_ref, down_ref, terms_ref, factors_ref, side_ref
):
    tokens = terms_ref.shape[0]
    width = down_ref.shape[1]
    tail = own_ref[2 * CAP :, :].astype(f32) + other_ref[2 * CAP :, :].astype(f32)
    square = tail[0:1, 2 * LANES : 3 * LANES] + tail[1:2, 2 * LANES : 3 * LANES]
    inverse = lax.rsqrt(square / D + epsilon)
    logits = (tail[:E, :LANES] + tail[:E, LANES : 2 * LANES]) * inverse
    every = iota((E, LANES), 0)
    picked = [
        jnp.sum(jnp.where(routes_ref[c : c + 1, :] == every, logits, 0.0), axis=0, keepdims=True)
        for c in range(2)
    ]
    top = jnp.maximum(picked[0], picked[1])
    raised = [jnp.exp(p - top) for p in picked]
    total = raised[0] + raised[1]
    shares = [r / total for r in raised]
    first = lax.axis_index("ep") * (2 * PAIRS)

    def factors_of(pair):
        slots = []
        for i in range(2):
            share = jnp.zeros((1, LANES), f32)
            for c in range(2):
                share = share + jnp.where(
                    routes_ref[c : c + 1, :] == first + 2 * pair + i, shares[c], 0.0
                )
            slots.append(jnp.broadcast_to(share, (CAP, LANES)))
        table = tables_ref[pair, : 2 * CAP, :].astype(f32)
        slot_inverse = jnp.sum(table * inverse, axis=1, keepdims=True)
        slot_share = jnp.sum(table * jnp.concatenate(slots, axis=0), axis=1, keepdims=True)
        return jnp.where(iota((2 * CAP, LANES), 1) == 0, slot_inverse, slot_share)

    factors_ref[...] = factors_of(1)
    mixed = spread_pair(own_ref, other_ref, factors_of(0), turned_ref[0], side_ref, tokens)
    terms_ref[...] = sum(
        jnp.dot(
            mixed[:, e * width : (e + 1) * width], down_ref[e], preferred_element_type=f32
        )
        for e in range(2)
    )


def down_rest_kernel(
    own_ref, other_ref, terms_ref, factors_ref, turned_ref, down_ref, out_ref, side_ref, wide_ref
):
    tokens = terms_ref.shape[0]
    width = down_ref.shape[1]
    blocks = down_ref.shape[2] // LANES
    stride = STEPS * blocks
    groups = tokens // STEPS
    mixed = spread_pair(own_ref, other_ref, factors_ref[...], turned_ref[1], side_ref, tokens)
    chunk = 4 * LANES
    for n in range(down_ref.shape[2] // chunk):
        terms = terms_ref[:, n * chunk : (n + 1) * chunk]
        for i in range(2):
            terms = terms + jnp.dot(
                mixed[:, i * width : (i + 1) * width],
                down_ref[2 + i, :, n * chunk : (n + 1) * chunk],
                preferred_element_type=f32,
            )
        for j in range(chunk // LANES):
            k = n * (chunk // LANES) + j
            for s in range(STEPS):
                wide_ref[pl.ds(k * STEPS + s, groups, stride=stride), :] = terms[
                    s * groups : (s + 1) * groups, j * LANES : (j + 1) * LANES
                ]
    out_ref[...] = wide_ref[...].astype(bf16)


def output_kernel(state_ref, own_ref, other_ref, out_ref, rows_ref):
    steps, width = out_ref.shape
    rows_ref[...] = state_ref[...].astype(f32) + (own_ref[...] + other_ref[...])
    for k in range(width // LANES):
        out_ref[:, k * LANES : (k + 1) * LANES] = rows_ref[k * steps : (k + 1) * steps, :].astype(
            bf16
        )


def on_device(
    queries,
    new_keys,
    new_values,
    cache_keys,
    cache_values,
    lengths,
    residual,
    out_weight,
    norm_gain,
    router_weight,
    routes,
    expert_gate,
    expert_up,
    expert_down,
):
    groups = lax.axis_size("grp")
    steps, _, query_width = queries.shape
    rows = steps * query_width // HD
    struct = jax.ShapeDtypeStruct
    token_count = groups * steps
    width = residual.shape[2]
    kv_width = cache_keys.shape[2]
    cached = cache_keys.shape[1]
    mask = call(mask_kernel, struct((8, cached), f32), (lengths,), [SMEM], beside=3)
    partial = call(
        attention_kernel,
        struct((rows, 2 * HD), bf16),
        (
            mask,
            queries.reshape(steps, query_width),
            cache_keys.reshape(cached, kv_width),
            cache_values.reshape(cached, kv_width),
            new_keys.reshape(steps, kv_width),
            new_values.reshape(steps, kv_width),
        ),
        [VMEM] * 6,
        [pltpu.VMEM((rows, HD), f32)],
        beside=2,
    )
    square = struct((PAIRS, LANES, LANES), bf16)
    residual_rows, routes_row, tables, turned = call(
        rows_kernel,
        (struct((rows, LANES), f32), struct((2, LANES), jnp.int32), square, square),
        (residual.reshape(steps, width), routes.transpose(0, 2, 1)),
        [VMEM] * 2,
    )
    other = lax.ppermute(partial, "tp", swap)
    attended = call(
        join_kernel,
        struct((steps, query_width), bf16),
        (partial, other),
        [VMEM] * 2,
        [pltpu.VMEM((rows, HD), f32)],
        beside=2,
    )
    terms = call(
        project_kernel,
        struct((rows, LANES), bf16),
        (attended, out_weight),
        [VMEM] * 2,
        [pltpu.VMEM((rows, LANES), f32)],
        beside=20,
    )
    other_terms = lax.ppermute(terms, "ep", swap)
    state = (residual_rows + (terms.astype(f32) + other_terms.astype(f32))).astype(bf16)
    all_state = lax.all_to_all(
        jnp.broadcast_to(state[None], (groups, rows, LANES)), "grp", 0, 0
    ).reshape(groups * rows, LANES)
    hidden_width = 2 * expert_gate.shape[2]
    both = pltpu.VMEM((2, LANES, hidden_width), bf16)
    sums = pltpu.VMEM((4, token_count, hidden_width // 2), f32)
    hidden, *scaled = call(
        hidden_kernel,
        (
            struct((2 * CAP + EXTRA, hidden_width), bf16),
            *[struct((token_count, width // PARTS), bf16)] * PARTS,
        ),
        (
            all_state,
            norm_gain.reshape(1, -1),
            router_weight.T,
            tables,
            expert_gate,
            expert_up,
        ),
        [VMEM] * 6,
        [pltpu.VMEM((groups * rows, LANES), f32), sums, both],
        limit=8,
    )
    other_hidden = lax.ppermute(hidden, "tp", swap)
    hidden_rest = call(
        hidden_rest_kernel,
        struct((2 * CAP, hidden_width), bf16),
        (*scaled, tables, expert_gate, expert_up),
        [VMEM] * (PARTS + 3),
        [sums, both],
    )
    other_hidden_rest = lax.ppermute(hidden_rest, "tp", swap)
    side = pltpu.VMEM((LANES, hidden_width), bf16)
    down_terms, factors = call(
        down_kernel,
        (struct((token_count, width), f32), struct((2 * CAP, LANES), f32)),
        (hidden, other_hidden, routes_row, tables, turned, expert_down),
        [VMEM] * 6,
        [side],
        limit=8,
    )
    sent = call(
        down_rest_kernel,
        struct((groups * rows, LANES), bf16),
        (hidden_rest, other_hidden_rest, down_terms, factors, turned, expert_down),
        [VMEM] * 6,
        [side, pltpu.VMEM((groups * rows, LANES), f32)],
        limit=8,
    )
    received = lax.all_to_all(sent.reshape(groups, rows, LANES), "grp", 0, 0)
    summed = jnp.sum(received.astype(f32), axis=0)
    other_summed = lax.ppermute(summed, "ep", swap)
    mixed = call(
        output_kernel,
        struct((steps, width), bf16),
        (state, summed, other_summed),
        [VMEM] * 3,
        [pltpu.VMEM((rows, LANES), f32)],
    )
    return mixed[:, None]


def solution(mesh):
    in_specs = (
        P(None, "grp", "ep"),
        P(None, "grp", "ep"),
        P(None, "grp", "ep"),
        P("grp", "tp", "ep"),
        P("grp", "tp", "ep"),
        P("grp"),
        P(None, "grp", "tp"),
        P("ep", "tp"),
        P("tp"),
        P("tp", None),
        P(),
        P("ep", "tp", "grp"),
        P("ep", "tp", "grp"),
        P("ep", "grp", "tp"),
    )
    out_specs = P(None, "grp", "tp")
    return jax.shard_map(
        on_device, mesh=mesh, in_specs=in_specs, out_specs=out_specs, check_vma=False
    )
```

```python
import functools

import jax
import jax.numpy as jnp
from jax import lax
from jax.experimental import pallas as pl
from jax.experimental.pallas import tpu as pltpu
from jax.sharding import PartitionSpec as P

D = 6144
HD = 128
E = 8
CAP = 48
PAIRS = 2
STEPS = 3
HALF_PARTS = 2
PIECE = 40
EXTRA = 16
LANES = 128

far_below = -1e30
epsilon = 1e-05
VMEM = pl.BlockSpec(memory_space=pltpu.VMEM)
SMEM = pl.BlockSpec(memory_space=pltpu.SMEM)
swap = [(0, 1), (1, 0)]
f32 = jnp.float32
bf16 = jnp.bfloat16


def call(kernel, out, operands, specs, scratch=(), limit=4, beside=0):
    return pl.pallas_call(
        kernel,
        out_shape=out,
        in_specs=specs,
        out_specs=jax.tree.map(lambda _: VMEM, out),
        scratch_shapes=scratch,
        compiler_params=pltpu.CompilerParams(vmem_limit_bytes=limit * 2**20),
        cost_estimate=pl.CostEstimate(
            flops=beside * 10**9, bytes_accessed=0, transcendentals=0
        )
        if beside
        else None,
    )(*operands)


def iota(shape, dim):
    return lax.broadcasted_iota(jnp.int32, shape, dim)


def pieces(value):
    high = value.astype(bf16).astype(f32)
    rest = value - high
    middle = rest.astype(bf16).astype(f32)
    return high, middle, rest - middle


def mask_kernel(length_ref, out_ref):
    cached = out_ref.shape[1]
    place = iota(out_ref.shape, 1) + lax.axis_index("tp") * cached
    out_ref[...] = jnp.where(place < length_ref[0], 1.0, 0.0)


def rows_kernel(residual_ref, routes_ref, rows_ref, routes_row_ref, tables_ref, turned_ref):
    steps, width = residual_ref.shape
    groups = routes_ref.shape[2]
    for k in range(width // LANES):
        rows_ref[k * steps : (k + 1) * steps, :] = residual_ref[
            :, k * LANES : (k + 1) * LANES
        ].astype(f32)
    routes_row_ref[...] = jnp.full(routes_row_ref.shape, -1, jnp.int32)
    for s in range(steps):
        routes_row_ref[:, s * groups : (s + 1) * groups] = routes_ref[s]
    count = E // 2
    wanted = iota((E, LANES), 0) + lax.axis_index("ep") * count
    ones = jnp.where(
        (routes_row_ref[0:1, :] == wanted) | (routes_row_ref[1:2, :] == wanted), 1.0, 0.0
    )
    earlier = jnp.where(iota((LANES, LANES), 0) < iota((LANES, LANES), 1), 1.0, 0.0)
    place = jnp.dot(
        ones.astype(bf16), earlier.astype(bf16), preferred_element_type=f32
    ).astype(jnp.int32)
    slot = iota((CAP, LANES), 0)
    for pair in range(PAIRS):
        table = jnp.concatenate(
            [
                jnp.where(place[e : e + 1, :] == slot, ones[e : e + 1, :], 0.0)
                for e in (2 * pair, 2 * pair + 1)
            ]
            + [jnp.zeros((LANES - 2 * CAP, LANES), f32)],
            axis=0,
        )
        tables_ref[pair] = table.astype(bf16)
        turned_ref[pair] = table.T.astype(bf16)


def attention_kernel(
    mask_ref, query_ref, key_ref, value_ref, new_key_ref, new_value_ref, out_ref, rows_ref
):
    steps = query_ref.shape[0]
    heads = query_ref.shape[1] // HD
    kv = key_ref.shape[1] // HD
    rows = heads * steps
    per_kv = rows // kv
    part = lax.axis_index("tp")
    for h in range(heads):
        rows_ref[h * steps : (h + 1) * steps, :] = query_ref[:, h * HD : (h + 1) * HD].astype(f32)
    query = rows_ref[...]
    row = iota((rows, 1), 0)
    owner = [(row >= k * per_kv) & (row < (k + 1) * per_kv) for k in range(kv)]
    step = row % steps
    scale = HD ** (-0.5)
    spread = jnp.concatenate(
        [jnp.where(owner[k], query, 0.0).astype(bf16) for k in range(kv)], axis=1
    )
    scores = (
        lax.dot_general(
            spread, key_ref[...], (((1,), (1,)), ((), ())), preferred_element_type=f32
        )
        * scale
    )
    allowed = mask_ref[0:1, :] > 0.0
    scores = jnp.where(allowed, scores, far_below)
    new_key = new_key_ref[...].astype(f32)

    def chosen(wide, t):
        out = jnp.zeros((rows, HD), f32)
        for k in range(kv):
            out = jnp.where(owner[k], wide[t : t + 1, k * HD : (k + 1) * HD], out)
        return out

    fresh_ok = [(step >= t) & (part == 0) for t in range(steps)]
    fresh = [
        jnp.where(
            fresh_ok[t],
            jnp.sum(query * chosen(new_key, t), axis=1, keepdims=True) * scale,
            far_below,
        )
        for t in range(steps)
    ]
    highest = jnp.max(scores, axis=1, keepdims=True)
    for t in range(steps):
        highest = jnp.maximum(highest, fresh[t])
    exponent = jnp.where(allowed, jnp.exp(scores - highest), 0.0)
    totals = jnp.sum(exponent, axis=1, keepdims=True)
    new_value = new_value_ref[...].astype(f32)
    wide = jnp.dot(exponent.astype(bf16), value_ref[...], preferred_element_type=f32)
    weighted = jnp.zeros((rows, HD), f32)
    for k in range(kv):
        weighted = jnp.where(owner[k], wide[:, k * HD : (k + 1) * HD], weighted)
    for t in range(steps):
        term = jnp.where(fresh_ok[t], jnp.exp(fresh[t] - highest), 0.0)
        totals = totals + term
        weighted = weighted + term.astype(bf16).astype(f32) * chosen(new_value, t)
    present = totals > 0.0
    safe = jnp.where(present, totals, 1.0)
    out_ref[:, :HD] = (weighted / safe).astype(bf16)
    tail = pieces(highest) + pieces(totals)
    lane = iota((rows, LANES), 1)
    row_tail = jnp.zeros((rows, LANES), f32)
    for i, piece in enumerate(tail):
        row_tail = jnp.where(lane == i, piece, row_tail)
    out_ref[:, HD:] = row_tail.astype(bf16)


def join_kernel(own_ref, other_ref, attended_ref, rows_ref):
    steps = attended_ref.shape[0]
    heads = own_ref.shape[0] // steps

    def read(ref):
        tail = ref[:, HD:].astype(f32)
        highest = tail[:, 0:1] + tail[:, 1:2] + tail[:, 2:3]
        totals = tail[:, 3:4] + tail[:, 4:5] + tail[:, 5:6]
        return ref[:, :HD].astype(f32), highest, totals

    own, own_highest, own_totals = read(own_ref)
    other, other_highest, other_totals = read(other_ref)
    top = jnp.maximum(own_highest, other_highest)
    own_factor = own_totals * jnp.exp(own_highest - top)
    other_factor = other_totals * jnp.exp(other_highest - top)
    rows_ref[...] = (own * own_factor + other * other_factor) / (own_factor + other_factor)
    attended_ref[...] = jnp.concatenate(
        [rows_ref[h * steps : (h + 1) * steps, :] for h in range(heads)], axis=1
    ).astype(bf16)


def project_kernel(attended_ref, weight_ref, out_ref, rows_ref):
    steps = attended_ref.shape[0]
    terms = jnp.dot(attended_ref[...], weight_ref[...], preferred_element_type=f32)
    for k in range(weight_ref.shape[1] // LANES):
        rows_ref[k * steps : (k + 1) * steps, :] = terms[:, k * LANES : (k + 1) * LANES]
    out_ref[...] = rows_ref[...].astype(bf16)


def state_kernel(residual_ref, own_ref, other_ref, state_ref, sent_ref, rows_ref, wide_ref):
    rows = state_ref.shape[0]
    half = rows // 2
    state = (
        residual_ref[...] + (own_ref[...].astype(f32) + other_ref[...].astype(f32))
    ).astype(bf16)
    state_ref[...] = state
    rows_ref[:rows, :] = state.astype(f32)
    rows_ref[rows:, :] = jnp.zeros((rows_ref.shape[0] - rows, LANES), f32)
    piece = jnp.where(
        lax.axis_index("ep") == 0, rows_ref[:PIECE, :], rows_ref[half : half + PIECE, :]
    )
    for g in range(wide_ref.shape[0] // PIECE):
        wide_ref[g * PIECE : (g + 1) * PIECE, :] = piece
    sent_ref[...] = wide_ref[...].astype(bf16)


def scale_half(first, state_ref, gain_ref, scaled_refs, wide_ref):
    part = scaled_refs[0].shape[1]
    groups = state_ref.shape[0] // PIECE
    wide_ref[...] = state_ref[...].astype(f32)
    squares = [jnp.zeros((groups, LANES), f32) for _ in range(STEPS)]
    for k in range(len(scaled_refs) * part // LANES):
        gain = gain_ref[:, pl.ds(pl.multiple_of(first + k * LANES, LANES), LANES)]
        scaled_ref = scaled_refs[k * LANES // part]
        column = k * LANES % part
        for s in range(STEPS):
            block = wide_ref[pl.ds(k * STEPS + s, groups, stride=PIECE), :]
            squares[s] = squares[s] + block * block
            scaled_ref[s * groups : (s + 1) * groups, column : column + LANES] = (
                block * gain
            ).astype(bf16)
    return jnp.concatenate(squares, axis=0)


def route_half(first, router_ref, scaled_refs):
    part = scaled_refs[0].shape[1]
    return sum(
        lax.dot_general(
            router_ref[:, pl.ds(pl.multiple_of(first + n * part, LANES), part)],
            ref[...],
            (((1,), (1,)), ((), ())),
            preferred_element_type=f32,
        )
        for n, ref in enumerate(scaled_refs)
    )


def add_half(first, pair, scaled_refs, gate_ref, up_ref, before_ref, sums_ref, put):
    part = scaled_refs[0].shape[1]
    last = len(scaled_refs) - 1
    for n, scaled_ref in enumerate(scaled_refs):
        scaled = scaled_ref[...]
        depth = pl.ds(pl.multiple_of(first + n * part, LANES), part)
        for i in range(2):
            for j, weight_ref in enumerate((gate_ref, up_ref)):
                terms = jnp.dot(
                    scaled, weight_ref[2 * pair + i, depth, :], preferred_element_type=f32
                )
                if n > 0:
                    terms = terms + sums_ref[2 * i + j]
                elif before_ref is not None:
                    terms = terms + before_ref[4 * pair + 2 * i + j]
                if n < last:
                    sums_ref[2 * i + j] = terms
                else:
                    put(i, j, terms)


def own_half_kernel(
    state_ref, gain_ref, router_ref, gate_ref, up_ref, terms_ref, square_ref, logits_ref, *refs
):
    *scaled_refs, wide_ref, sums_ref = refs
    first = lax.axis_index("ep") * (len(scaled_refs) * scaled_refs[0].shape[1])
    square_ref[...] = scale_half(first, state_ref, gain_ref, scaled_refs, wide_ref)
    for pair in range(PAIRS):

        def put(i, j, terms, pair=pair):
            terms_ref[4 * pair + 2 * i + j] = terms

        add_half(first, pair, scaled_refs, gate_ref, up_ref, None, sums_ref, put)
    logits_ref[...] = route_half(first, router_ref, scaled_refs)


def pack_pair(
    first, pair, scaled_refs, tables_ref, gate_ref, up_ref, terms_ref, out_ref, sums_ref, both_ref
):
    tokens = scaled_refs[0].shape[0]
    width = gate_ref.shape[2]
    both_ref[:, tokens:, :] = jnp.zeros((2, LANES - tokens, 2 * width), bf16)

    def put(i, j, terms):
        both_ref[i, :tokens, j * width : (j + 1) * width] = terms.astype(bf16)

    add_half(first, pair, scaled_refs, gate_ref, up_ref, terms_ref, sums_ref, put)
    for i in range(2):
        out_ref[i * CAP : (i + 1) * CAP, :] = jnp.dot(
            tables_ref[pair, i * CAP : (i + 1) * CAP, :],
            both_ref[i],
            preferred_element_type=f32,
        ).astype(bf16)


def hidden_kernel(
    state_ref,
    gain_ref,
    router_ref,
    tables_ref,
    gate_ref,
    up_ref,
    terms_ref,
    square_ref,
    logits_ref,
    out_ref,
    *refs,
):
    *scaled_refs, wide_ref, sums_ref, both_ref = refs
    tokens = scaled_refs[0].shape[0]
    first = (1 - lax.axis_index("ep")) * (len(scaled_refs) * scaled_refs[0].shape[1])
    squares = square_ref[...] + scale_half(first, state_ref, gain_ref, scaled_refs, wide_ref)
    pack_pair(
        first, 0, scaled_refs, tables_ref, gate_ref, up_ref, terms_ref, out_ref, sums_ref, both_ref
    )
    square = jnp.sum(squares, axis=1, keepdims=True)
    diagonal = iota((tokens, LANES), 0) == iota((tokens, LANES), 1)
    square = jnp.sum(jnp.where(diagonal, square, 0.0), axis=0, keepdims=True)
    router = logits_ref[...] + route_half(first, router_ref, scaled_refs)
    router = jnp.concatenate([router, jnp.zeros((E, LANES - tokens), f32)], axis=1)
    high, middle, _ = pieces(router)
    square_high, square_middle, _ = pieces(square)
    line = iota((E, LANES), 0)
    extra = jnp.concatenate(
        [
            high,
            middle,
            jnp.where(line == 0, square_high, jnp.where(line == 1, square_middle, 0.0)),
            jnp.zeros((E, LANES), f32),
        ],
        axis=1,
    )
    extra = jnp.concatenate([extra, jnp.zeros((EXTRA - E, 4 * LANES), f32)], axis=0)
    out_ref[2 * CAP :, :] = extra.astype(bf16)


def hidden_rest_kernel(*refs):
    *scaled_refs, tables_ref, gate_ref, up_ref, terms_ref, out_ref, sums_ref, both_ref = refs
    first = (1 - lax.axis_index("ep")) * (len(scaled_refs) * scaled_refs[0].shape[1])
    pack_pair(
        first, 1, scaled_refs, tables_ref, gate_ref, up_ref, terms_ref, out_ref, sums_ref, both_ref
    )


def spread_pair(own_ref, other_ref, factors, turned, side_ref, tokens):
    width = side_ref.shape[1] // 2
    side_ref[...] = jnp.zeros(side_ref.shape, bf16)
    both = own_ref[: 2 * CAP, :].astype(f32) + other_ref[: 2 * CAP, :].astype(f32)
    both = both * factors[:, 0:1]
    gate, up = both[:, :width], both[:, width:]
    activated = (gate / (1.0 + jnp.exp(-gate)) * up).astype(bf16).astype(f32)
    weighted = (activated * factors[:, 1:2]).astype(bf16)
    for i in range(2):
        side_ref[i * CAP : (i + 1) * CAP, i * width : (i + 1) * width] = weighted[
            i * CAP : (i + 1) * CAP, :
        ]
    return jnp.dot(turned[:tokens, :], side_ref[...], preferred_element_type=f32).astype(bf16)


def down_kernel(
    own_ref, other_ref, routes_ref, tables_ref, turned_ref, down_ref, terms_ref, factors_ref, side_ref
):
    tokens = terms_ref.shape[0]
    width = down_ref.shape[1]
    tail = own_ref[2 * CAP :, :].astype(f32) + other_ref[2 * CAP :, :].astype(f32)
    square = tail[0:1, 2 * LANES : 3 * LANES] + tail[1:2, 2 * LANES : 3 * LANES]
    inverse = lax.rsqrt(square / D + epsilon)
    logits = (tail[:E, :LANES] + tail[:E, LANES : 2 * LANES]) * inverse
    every = iota((E, LANES), 0)
    picked = [
        jnp.sum(jnp.where(routes_ref[c : c + 1, :] == every, logits, 0.0), axis=0, keepdims=True)
        for c in range(2)
    ]
    top = jnp.maximum(picked[0], picked[1])
    raised = [jnp.exp(p - top) for p in picked]
    total = raised[0] + raised[1]
    shares = [r / total for r in raised]
    first = lax.axis_index("ep") * (2 * PAIRS)

    def factors_of(pair):
        slots = []
        for i in range(2):
            share = jnp.zeros((1, LANES), f32)
            for c in range(2):
                share = share + jnp.where(
                    routes_ref[c : c + 1, :] == first + 2 * pair + i, shares[c], 0.0
                )
            slots.append(jnp.broadcast_to(share, (CAP, LANES)))
        table = tables_ref[pair, : 2 * CAP, :].astype(f32)
        slot_inverse = jnp.sum(table * inverse, axis=1, keepdims=True)
        slot_share = jnp.sum(table * jnp.concatenate(slots, axis=0), axis=1, keepdims=True)
        return jnp.where(iota((2 * CAP, LANES), 1) == 0, slot_inverse, slot_share)

    factors_ref[...] = factors_of(1)
    mixed = spread_pair(own_ref, other_ref, factors_of(0), turned_ref[0], side_ref, tokens)
    terms_ref[...] = sum(
        jnp.dot(
            mixed[:, e * width : (e + 1) * width], down_ref[e], preferred_element_type=f32
        )
        for e in range(2)
    )


def half_terms(first, mixed, terms_ref, down_ref, width, put):
    depth = down_ref.shape[1]
    chunk = 4 * LANES
    for n in range(width // chunk):
        columns = pl.ds(pl.multiple_of(first + n * chunk, LANES), chunk)
        terms = terms_ref[:, columns]
        for i in range(2):
            terms = terms + jnp.dot(
                mixed[:, i * depth : (i + 1) * depth],
                down_ref[2 + i, :, columns],
                preferred_element_type=f32,
            )
        put(n * chunk, terms)


def down_away_kernel(
    own_ref, other_ref, terms_ref, factors_ref, turned_ref, down_ref, away_ref, mixed_ref, side_ref
):
    tokens, width = away_ref.shape
    mixed = spread_pair(own_ref, other_ref, factors_ref[...], turned_ref[1], side_ref, tokens)
    mixed_ref[...] = mixed

    def put(column, terms):
        away_ref[:, column : column + terms.shape[1]] = terms.astype(bf16)

    first = (1 - lax.axis_index("ep")) * width
    half_terms(first, mixed, terms_ref, down_ref, width, put)


def down_here_kernel(mixed_ref, terms_ref, down_ref, here_ref):
    width = here_ref.shape[1]

    def put(column, terms):
        here_ref[:, column : column + terms.shape[1]] = terms

    half_terms(lax.axis_index("ep") * width, mixed_ref[...], terms_ref, down_ref, width, put)


def send_kernel(here_ref, came_ref, out_ref, wide_ref):
    groups = here_ref.shape[0] // STEPS
    blocks = here_ref.shape[1] // LANES
    wide_ref[...] = jnp.zeros(wide_ref.shape, f32)
    for k in range(blocks):
        columns = slice(k * LANES, (k + 1) * LANES)
        for s in range(STEPS):
            tokens = slice(s * groups, (s + 1) * groups)
            wide_ref[pl.ds(k * STEPS + s, groups, stride=PIECE), :] = here_ref[
                tokens, columns
            ] + came_ref[tokens, columns].astype(f32)
    out_ref[...] = wide_ref[...].astype(bf16)


def output_kernel(state_ref, own_ref, other_ref, out_ref, rows_ref):
    steps, width = out_ref.shape
    half = state_ref.shape[0] // 2
    lower = lax.axis_index("ep") == 0
    own, other = own_ref[...], other_ref[...]
    rows_ref[:PIECE, :] = jnp.where(lower, own, other)
    rows_ref[half : half + PIECE, :] = jnp.where(lower, other, own)
    rows_ref[: 2 * half, :] = state_ref[...].astype(f32) + rows_ref[: 2 * half, :]
    for k in range(width // LANES):
        out_ref[:, k * LANES : (k + 1) * LANES] = rows_ref[k * steps : (k + 1) * steps, :].astype(
            bf16
        )


def on_device(
    queries,
    new_keys,
    new_values,
    cache_keys,
    cache_values,
    lengths,
    residual,
    out_weight,
    norm_gain,
    router_weight,
    routes,
    expert_gate,
    expert_up,
    expert_down,
):
    groups = lax.axis_size("grp")
    steps, _, query_width = queries.shape
    rows = steps * query_width // HD
    struct = jax.ShapeDtypeStruct
    token_count = groups * steps
    width = residual.shape[2]
    kv_width = cache_keys.shape[2]
    cached = cache_keys.shape[1]
    mask = call(mask_kernel, struct((8, cached), f32), (lengths,), [SMEM], beside=3)
    partial = call(
        attention_kernel,
        struct((rows, 2 * HD), bf16),
        (
            mask,
            queries.reshape(steps, query_width),
            cache_keys.reshape(cached, kv_width),
            cache_values.reshape(cached, kv_width),
            new_keys.reshape(steps, kv_width),
            new_values.reshape(steps, kv_width),
        ),
        [VMEM] * 6,
        [pltpu.VMEM((rows, HD), f32)],
        beside=2,
    )
    square = struct((PAIRS, LANES, LANES), bf16)
    residual_rows, routes_row, tables, turned = call(
        rows_kernel,
        (struct((rows, LANES), f32), struct((2, LANES), jnp.int32), square, square),
        (residual.reshape(steps, width), routes.transpose(0, 2, 1)),
        [VMEM] * 2,
    )
    other = lax.ppermute(partial, "tp", swap)
    attended = call(
        join_kernel,
        struct((steps, query_width), bf16),
        (partial, other),
        [VMEM] * 2,
        [pltpu.VMEM((rows, HD), f32)],
        beside=2,
    )
    terms = call(
        project_kernel,
        struct((rows, LANES), bf16),
        (attended, out_weight),
        [VMEM] * 2,
        [pltpu.VMEM((rows, LANES), f32)],
        beside=20,
    )
    other_terms = lax.ppermute(terms, "ep", swap)
    state, sent_state = call(
        state_kernel,
        (struct((rows, LANES), bf16), struct((groups * PIECE, LANES), bf16)),
        (residual_rows, terms, other_terms),
        [VMEM] * 3,
        [pltpu.VMEM((2 * PIECE, LANES), f32), pltpu.VMEM((groups * PIECE, LANES), f32)],
    )
    own_state = lax.all_to_all(
        sent_state.reshape(groups, PIECE, LANES), "grp", 0, 0
    ).reshape(groups * PIECE, LANES)
    other_state = lax.ppermute(own_state, "ep", swap)
    gain = norm_gain.reshape(1, -1)
    router = router_weight.T
    expert_width = expert_gate.shape[2]
    hidden_width = 2 * expert_width
    part = (token_count, width // (2 * HALF_PARTS))
    wide = pltpu.VMEM((groups * PIECE, LANES), f32)
    sums = pltpu.VMEM((4, token_count, expert_width), f32)
    both = pltpu.VMEM((2, LANES, hidden_width), bf16)
    own_terms, squares, logits = call(
        own_half_kernel,
        (
            struct((4 * PAIRS, token_count, expert_width), f32),
            struct((token_count, LANES), f32),
            struct((E, token_count), f32),
        ),
        (own_state, gain, router, expert_gate, expert_up),
        [VMEM] * 5,
        [pltpu.VMEM(part, bf16)] * HALF_PARTS + [wide, sums],
    )
    hidden, *scaled = call(
        hidden_kernel,
        (
            struct((2 * CAP + EXTRA, hidden_width), bf16),
            *[struct(part, bf16)] * HALF_PARTS,
        ),
        (
            other_state,
            gain,
            router,
            tables,
            expert_gate,
            expert_up,
            own_terms,
            squares,
            logits,
        ),
        [VMEM] * 9,
        [wide, sums, both],
    )
    other_hidden = lax.ppermute(hidden, "tp", swap)
    hidden_rest = call(
        hidden_rest_kernel,
        struct((2 * CAP, hidden_width), bf16),
        (*scaled, tables, expert_gate, expert_up, own_terms),
        [VMEM] * (HALF_PARTS + 4),
        [sums, both],
    )
    other_hidden_rest = lax.ppermute(hidden_rest, "tp", swap)
    side = pltpu.VMEM((LANES, hidden_width), bf16)
    down_terms, factors = call(
        down_kernel,
        (struct((token_count, width), f32), struct((2 * CAP, LANES), f32)),
        (hidden, other_hidden, routes_row, tables, turned, expert_down),
        [VMEM] * 6,
        [side],
        limit=8,
    )
    half = width // 2
    away, spread = call(
        down_away_kernel,
        (struct((token_count, half), bf16), struct((token_count, hidden_width), bf16)),
        (hidden_rest, other_hidden_rest, down_terms, factors, turned, expert_down),
        [VMEM] * 6,
        [side],
    )
    came = lax.ppermute(away, "ep", swap)
    here = call(
        down_here_kernel,
        struct((token_count, half), f32),
        (spread, down_terms, expert_down),
        [VMEM] * 3,
    )
    sent = call(
        send_kernel,
        struct((groups * PIECE, LANES), bf16),
        (here, came),
        [VMEM] * 2,
        [wide],
    )
    received = lax.all_to_all(sent.reshape(groups, PIECE, LANES), "grp", 0, 0)
    summed = jnp.sum(received.astype(f32), axis=0)
    other_summed = lax.ppermute(summed, "ep", swap)
    mixed = call(
        output_kernel,
        struct((steps, width), bf16),
        (state, summed, other_summed),
        [VMEM] * 3,
        [pltpu.VMEM((2 * PIECE, LANES), f32)],
    )
    return mixed[:, None]


def solution(mesh):
    in_specs = (
        P(None, "grp", "ep"),
        P(None, "grp", "ep"),
        P(None, "grp", "ep"),
        P("grp", "tp", "ep"),
        P("grp", "tp", "ep"),
        P("grp"),
        P(None, "grp", "tp"),
        P("ep", "tp"),
        P("tp"),
        P("tp", None),
        P(),
        P("ep", "tp", "grp"),
        P("ep", "tp", "grp"),
        P("ep", "grp", "tp"),
    )
    out_specs = P(None, "grp", "tp")
    return jax.shard_map(
        on_device, mesh=mesh, in_specs=in_specs, out_specs=out_specs, check_vma=False
    )
```

```python
import functools

import jax
import jax.numpy as jnp
from jax import lax
from jax.experimental import pallas as pl
from jax.experimental.pallas import tpu as pltpu
from jax.sharding import PartitionSpec as P

D = 6144
HD = 128
E = 8
CAP = 48
PAIRS = 2
STEPS = 3
HALF_PARTS = 2
HALF_ROWS = 36
PIECE = 40
EXTRA = 16
LANES = 128

far_below = -1e30
epsilon = 1e-05
VMEM = pl.BlockSpec(memory_space=pltpu.VMEM)
SMEM = pl.BlockSpec(memory_space=pltpu.SMEM)
swap = [(0, 1), (1, 0)]
f32 = jnp.float32
bf16 = jnp.bfloat16


def call(kernel, out, operands, specs, scratch=(), limit=4, beside=0):
    return pl.pallas_call(
        kernel,
        out_shape=out,
        in_specs=specs,
        out_specs=jax.tree.map(lambda _: VMEM, out),
        scratch_shapes=scratch,
        compiler_params=pltpu.CompilerParams(vmem_limit_bytes=limit * 2**20),
        cost_estimate=pl.CostEstimate(
            flops=beside * 10**9, bytes_accessed=0, transcendentals=0
        )
        if beside
        else None,
    )(*operands)


def iota(shape, dim):
    return lax.broadcasted_iota(jnp.int32, shape, dim)


def pieces(value):
    high = value.astype(bf16).astype(f32)
    rest = value - high
    middle = rest.astype(bf16).astype(f32)
    return high, middle, rest - middle


def mask_kernel(length_ref, out_ref):
    cached = out_ref.shape[1]
    place = iota(out_ref.shape, 1) + lax.axis_index("tp") * cached
    out_ref[...] = jnp.where(place < length_ref[0], 1.0, 0.0)


def rows_kernel(residual_ref, routes_ref, rows_ref, routes_row_ref, tables_ref, turned_ref):
    steps, width = residual_ref.shape
    groups = routes_ref.shape[2]
    for k in range(width // LANES):
        rows_ref[k * steps : (k + 1) * steps, :] = residual_ref[
            :, k * LANES : (k + 1) * LANES
        ].astype(f32)
    used = steps * width // LANES
    rows_ref[used:, :] = jnp.zeros((rows_ref.shape[0] - used, LANES), f32)
    routes_row_ref[...] = jnp.full(routes_row_ref.shape, -1, jnp.int32)
    for s in range(steps):
        routes_row_ref[:, s * groups : (s + 1) * groups] = routes_ref[s]
    count = E // 2
    wanted = iota((E, LANES), 0) + lax.axis_index("ep") * count
    ones = jnp.where(
        (routes_row_ref[0:1, :] == wanted) | (routes_row_ref[1:2, :] == wanted), 1.0, 0.0
    )
    earlier = jnp.where(iota((LANES, LANES), 0) < iota((LANES, LANES), 1), 1.0, 0.0)
    place = jnp.dot(
        ones.astype(bf16), earlier.astype(bf16), preferred_element_type=f32
    ).astype(jnp.int32)
    slot = iota((CAP, LANES), 0)
    for pair in range(PAIRS):
        table = jnp.concatenate(
            [
                jnp.where(place[e : e + 1, :] == slot, ones[e : e + 1, :], 0.0)
                for e in (2 * pair, 2 * pair + 1)
            ]
            + [jnp.zeros((LANES - 2 * CAP, LANES), f32)],
            axis=0,
        )
        tables_ref[pair] = table.astype(bf16)
        turned_ref[pair] = table.T.astype(bf16)


def attention_kernel(
    mask_ref, query_ref, key_ref, value_ref, new_key_ref, new_value_ref, out_ref, rows_ref
):
    steps = query_ref.shape[0]
    heads = query_ref.shape[1] // HD
    kv = key_ref.shape[1] // HD
    rows = heads * steps
    per_kv = rows // kv
    part = lax.axis_index("tp")
    for h in range(heads):
        rows_ref[h * steps : (h + 1) * steps, :] = query_ref[:, h * HD : (h + 1) * HD].astype(f32)
    query = rows_ref[...]
    row = iota((rows, 1), 0)
    owner = [(row >= k * per_kv) & (row < (k + 1) * per_kv) for k in range(kv)]
    step = row % steps
    scale = HD ** (-0.5)
    spread = jnp.concatenate(
        [jnp.where(owner[k], query, 0.0).astype(bf16) for k in range(kv)], axis=1
    )
    scores = (
        lax.dot_general(
            spread, key_ref[...], (((1,), (1,)), ((), ())), preferred_element_type=f32
        )
        * scale
    )
    allowed = mask_ref[0:1, :] > 0.0
    scores = jnp.where(allowed, scores, far_below)
    new_key = new_key_ref[...].astype(f32)

    def chosen(wide, t):
        out = jnp.zeros((rows, HD), f32)
        for k in range(kv):
            out = jnp.where(owner[k], wide[t : t + 1, k * HD : (k + 1) * HD], out)
        return out

    fresh_ok = [(step >= t) & (part == 0) for t in range(steps)]
    fresh = [
        jnp.where(
            fresh_ok[t],
            jnp.sum(query * chosen(new_key, t), axis=1, keepdims=True) * scale,
            far_below,
        )
        for t in range(steps)
    ]
    highest = jnp.max(scores, axis=1, keepdims=True)
    for t in range(steps):
        highest = jnp.maximum(highest, fresh[t])
    exponent = jnp.where(allowed, jnp.exp(scores - highest), 0.0)
    totals = jnp.sum(exponent, axis=1, keepdims=True)
    new_value = new_value_ref[...].astype(f32)
    wide = jnp.dot(exponent.astype(bf16), value_ref[...], preferred_element_type=f32)
    weighted = jnp.zeros((rows, HD), f32)
    for k in range(kv):
        weighted = jnp.where(owner[k], wide[:, k * HD : (k + 1) * HD], weighted)
    for t in range(steps):
        term = jnp.where(fresh_ok[t], jnp.exp(fresh[t] - highest), 0.0)
        totals = totals + term
        weighted = weighted + term.astype(bf16).astype(f32) * chosen(new_value, t)
    present = totals > 0.0
    safe = jnp.where(present, totals, 1.0)
    out_ref[:, :HD] = (weighted / safe).astype(bf16)
    tail = pieces(highest) + pieces(totals)
    lane = iota((rows, LANES), 1)
    row_tail = jnp.zeros((rows, LANES), f32)
    for i, piece in enumerate(tail):
        row_tail = jnp.where(lane == i, piece, row_tail)
    out_ref[:, HD:] = row_tail.astype(bf16)


def join_kernel(own_ref, other_ref, attended_ref, rows_ref):
    steps = attended_ref.shape[0]
    heads = own_ref.shape[0] // steps

    def read(ref):
        tail = ref[:, HD:].astype(f32)
        highest = tail[:, 0:1] + tail[:, 1:2] + tail[:, 2:3]
        totals = tail[:, 3:4] + tail[:, 4:5] + tail[:, 5:6]
        return ref[:, :HD].astype(f32), highest, totals

    own, own_highest, own_totals = read(own_ref)
    other, other_highest, other_totals = read(other_ref)
    top = jnp.maximum(own_highest, other_highest)
    own_factor = own_totals * jnp.exp(own_highest - top)
    other_factor = other_totals * jnp.exp(other_highest - top)
    rows_ref[...] = (own * own_factor + other * other_factor) / (own_factor + other_factor)
    attended_ref[...] = jnp.concatenate(
        [rows_ref[h * steps : (h + 1) * steps, :] for h in range(heads)], axis=1
    ).astype(bf16)


def project_kernel(away, attended_ref, weight_ref, out_ref, rows_ref):
    steps = attended_ref.shape[0]
    width = weight_ref.shape[1] // 2
    half = lax.axis_index("ep")
    if away:
        half = 1 - half
    columns = pl.ds(pl.multiple_of(half * width, LANES), width)
    terms = jnp.dot(attended_ref[...], weight_ref[:, columns], preferred_element_type=f32)
    used = steps * width // LANES
    rows_ref[used:, :] = jnp.zeros((rows_ref.shape[0] - used, LANES), f32)
    for k in range(width // LANES):
        rows_ref[k * steps : (k + 1) * steps, :] = terms[:, k * LANES : (k + 1) * LANES]
    out_ref[...] = rows_ref[...].astype(out_ref.dtype)


def state_kernel(residual_ref, here_ref, came_ref, state_ref, sent_ref, wide_ref):
    residual = jnp.where(
        lax.axis_index("ep") == 0,
        residual_ref[:PIECE, :],
        residual_ref[HALF_ROWS : HALF_ROWS + PIECE, :],
    )
    state = (residual + (here_ref[...] + came_ref[...].astype(f32))).astype(bf16).astype(f32)
    state_ref[...] = state
    for g in range(wide_ref.shape[0] // PIECE):
        wide_ref[g * PIECE : (g + 1) * PIECE, :] = state
    sent_ref[...] = wide_ref[...].astype(bf16)


def scale_half(first, state_ref, gain_ref, scaled_refs, wide_ref):
    part = scaled_refs[0].shape[1]
    groups = state_ref.shape[0] // PIECE
    wide_ref[...] = state_ref[...].astype(f32)
    squares = [jnp.zeros((groups, LANES), f32) for _ in range(STEPS)]
    for k in range(len(scaled_refs) * part // LANES):
        gain = gain_ref[:, pl.ds(pl.multiple_of(first + k * LANES, LANES), LANES)]
        scaled_ref = scaled_refs[k * LANES // part]
        column = k * LANES % part
        for s in range(STEPS):
            block = wide_ref[pl.ds(k * STEPS + s, groups, stride=PIECE), :]
            squares[s] = squares[s] + block * block
            scaled_ref[s * groups : (s + 1) * groups, column : column + LANES] = (
                block * gain
            ).astype(bf16)
    return jnp.concatenate(squares, axis=0)


def route_half(first, router_ref, scaled_refs):
    part = scaled_refs[0].shape[1]
    return sum(
        lax.dot_general(
            router_ref[:, pl.ds(pl.multiple_of(first + n * part, LANES), part)],
            ref[...],
            (((1,), (1,)), ((), ())),
            preferred_element_type=f32,
        )
        for n, ref in enumerate(scaled_refs)
    )


def add_half(first, pair, scaled_refs, gate_ref, up_ref, before_ref, sums_ref, put):
    part = scaled_refs[0].shape[1]
    last = len(scaled_refs) - 1
    for n, scaled_ref in enumerate(scaled_refs):
        scaled = scaled_ref[...]
        depth = pl.ds(pl.multiple_of(first + n * part, LANES), part)
        for i in range(2):
            for j, weight_ref in enumerate((gate_ref, up_ref)):
                terms = jnp.dot(
                    scaled, weight_ref[2 * pair + i, depth, :], preferred_element_type=f32
                )
                if n > 0:
                    terms = terms + sums_ref[2 * i + j]
                elif before_ref is not None:
                    terms = terms + before_ref[4 * pair + 2 * i + j]
                if n < last:
                    sums_ref[2 * i + j] = terms
                else:
                    put(i, j, terms)


def own_half_kernel(
    state_ref, gain_ref, router_ref, gate_ref, up_ref, terms_ref, square_ref, logits_ref, *refs
):
    *scaled_refs, wide_ref, sums_ref = refs
    first = lax.axis_index("ep") * (len(scaled_refs) * scaled_refs[0].shape[1])
    square_ref[...] = scale_half(first, state_ref, gain_ref, scaled_refs, wide_ref)
    for pair in range(PAIRS):

        def put(i, j, terms, pair=pair):
            terms_ref[4 * pair + 2 * i + j] = terms

        add_half(first, pair, scaled_refs, gate_ref, up_ref, None, sums_ref, put)
    logits_ref[...] = route_half(first, router_ref, scaled_refs)


def pack_pair(
    first, pair, scaled_refs, tables_ref, gate_ref, up_ref, terms_ref, out_ref, sums_ref, both_ref
):
    tokens = scaled_refs[0].shape[0]
    width = gate_ref.shape[2]
    both_ref[:, tokens:, :] = jnp.zeros((2, LANES - tokens, 2 * width), bf16)

    def put(i, j, terms):
        both_ref[i, :tokens, j * width : (j + 1) * width] = terms.astype(bf16)

    add_half(first, pair, scaled_refs, gate_ref, up_ref, terms_ref, sums_ref, put)
    for i in range(2):
        out_ref[i * CAP : (i + 1) * CAP, :] = jnp.dot(
            tables_ref[pair, i * CAP : (i + 1) * CAP, :],
            both_ref[i],
            preferred_element_type=f32,
        ).astype(bf16)


def hidden_kernel(
    state_ref,
    gain_ref,
    router_ref,
    tables_ref,
    gate_ref,
    up_ref,
    terms_ref,
    square_ref,
    logits_ref,
    out_ref,
    *refs,
):
    *scaled_refs, wide_ref, sums_ref, both_ref = refs
    tokens = scaled_refs[0].shape[0]
    first = (1 - lax.axis_index("ep")) * (len(scaled_refs) * scaled_refs[0].shape[1])
    squares = square_ref[...] + scale_half(first, state_ref, gain_ref, scaled_refs, wide_ref)
    pack_pair(
        first, 0, scaled_refs, tables_ref, gate_ref, up_ref, terms_ref, out_ref, sums_ref, both_ref
    )
    square = jnp.sum(squares, axis=1, keepdims=True)
    diagonal = iota((tokens, LANES), 0) == iota((tokens, LANES), 1)
    square = jnp.sum(jnp.where(diagonal, square, 0.0), axis=0, keepdims=True)
    router = logits_ref[...] + route_half(first, router_ref, scaled_refs)
    router = jnp.concatenate([router, jnp.zeros((E, LANES - tokens), f32)], axis=1)
    high, middle, _ = pieces(router)
    square_high, square_middle, _ = pieces(square)
    line = iota((E, LANES), 0)
    extra = jnp.concatenate(
        [
            high,
            middle,
            jnp.where(line == 0, square_high, jnp.where(line == 1, square_middle, 0.0)),
            jnp.zeros((E, LANES), f32),
        ],
        axis=1,
    )
    extra = jnp.concatenate([extra, jnp.zeros((EXTRA - E, 4 * LANES), f32)], axis=0)
    out_ref[2 * CAP :, :] = extra.astype(bf16)


def hidden_rest_kernel(*refs):
    *scaled_refs, tables_ref, gate_ref, up_ref, terms_ref, out_ref, sums_ref, both_ref = refs
    first = (1 - lax.axis_index("ep")) * (len(scaled_refs) * scaled_refs[0].shape[1])
    pack_pair(
        first, 1, scaled_refs, tables_ref, gate_ref, up_ref, terms_ref, out_ref, sums_ref, both_ref
    )


def spread_pair(own_ref, other_ref, factors, turned, side_ref, tokens):
    width = side_ref.shape[1] // 2
    side_ref[...] = jnp.zeros(side_ref.shape, bf16)
    both = own_ref[: 2 * CAP, :].astype(f32) + other_ref[: 2 * CAP, :].astype(f32)
    both = both * factors[:, 0:1]
    gate, up = both[:, :width], both[:, width:]
    activated = (gate / (1.0 + jnp.exp(-gate)) * up).astype(bf16).astype(f32)
    weighted = (activated * factors[:, 1:2]).astype(bf16)
    for i in range(2):
        side_ref[i * CAP : (i + 1) * CAP, i * width : (i + 1) * width] = weighted[
            i * CAP : (i + 1) * CAP, :
        ]
    return jnp.dot(turned[:tokens, :], side_ref[...], preferred_element_type=f32).astype(bf16)


def down_kernel(
    own_ref, other_ref, routes_ref, tables_ref, turned_ref, down_ref, terms_ref, factors_ref, side_ref
):
    tokens = terms_ref.shape[0]
    width = down_ref.shape[1]
    tail = own_ref[2 * CAP :, :].astype(f32) + other_ref[2 * CAP :, :].astype(f32)
    square = tail[0:1, 2 * LANES : 3 * LANES] + tail[1:2, 2 * LANES : 3 * LANES]
    inverse = lax.rsqrt(square / D + epsilon)
    logits = (tail[:E, :LANES] + tail[:E, LANES : 2 * LANES]) * inverse
    every = iota((E, LANES), 0)
    picked = [
        jnp.sum(jnp.where(routes_ref[c : c + 1, :] == every, logits, 0.0), axis=0, keepdims=True)
        for c in range(2)
    ]
    top = jnp.maximum(picked[0], picked[1])
    raised = [jnp.exp(p - top) for p in picked]
    total = raised[0] + raised[1]
    shares = [r / total for r in raised]
    first = lax.axis_index("ep") * (2 * PAIRS)

    def factors_of(pair):
        slots = []
        for i in range(2):
            share = jnp.zeros((1, LANES), f32)
            for c in range(2):
                share = share + jnp.where(
                    routes_ref[c : c + 1, :] == first + 2 * pair + i, shares[c], 0.0
                )
            slots.append(jnp.broadcast_to(share, (CAP, LANES)))
        table = tables_ref[pair, : 2 * CAP, :].astype(f32)
        slot_inverse = jnp.sum(table * inverse, axis=1, keepdims=True)
        slot_share = jnp.sum(table * jnp.concatenate(slots, axis=0), axis=1, keepdims=True)
        return jnp.where(iota((2 * CAP, LANES), 1) == 0, slot_inverse, slot_share)

    factors_ref[...] = factors_of(1)
    mixed = spread_pair(own_ref, other_ref, factors_of(0), turned_ref[0], side_ref, tokens)
    terms_ref[...] = sum(
        jnp.dot(
            mixed[:, e * width : (e + 1) * width], down_ref[e], preferred_element_type=f32
        )
        for e in range(2)
    )


def half_terms(first, mixed, terms_ref, down_ref, width, put):
    depth = down_ref.shape[1]
    chunk = 4 * LANES
    for n in range(width // chunk):
        columns = pl.ds(pl.multiple_of(first + n * chunk, LANES), chunk)
        terms = terms_ref[:, columns]
        for i in range(2):
            terms = terms + jnp.dot(
                mixed[:, i * depth : (i + 1) * depth],
                down_ref[2 + i, :, columns],
                preferred_element_type=f32,
            )
        put(n * chunk, terms)


def down_away_kernel(
    own_ref, other_ref, terms_ref, factors_ref, turned_ref, down_ref, away_ref, mixed_ref, side_ref
):
    tokens, width = away_ref.shape
    mixed = spread_pair(own_ref, other_ref, factors_ref[...], turned_ref[1], side_ref, tokens)
    mixed_ref[...] = mixed

    def put(column, terms):
        away_ref[:, column : column + terms.shape[1]] = terms.astype(bf16)

    first = (1 - lax.axis_index("ep")) * width
    half_terms(first, mixed, terms_ref, down_ref, width, put)


def down_here_kernel(mixed_ref, terms_ref, down_ref, here_ref):
    width = here_ref.shape[1]

    def put(column, terms):
        here_ref[:, column : column + terms.shape[1]] = terms

    half_terms(lax.axis_index("ep") * width, mixed_ref[...], terms_ref, down_ref, width, put)


def send_kernel(here_ref, came_ref, out_ref, wide_ref):
    groups = here_ref.shape[0] // STEPS
    blocks = here_ref.shape[1] // LANES
    wide_ref[...] = jnp.zeros(wide_ref.shape, f32)
    for k in range(blocks):
        columns = slice(k * LANES, (k + 1) * LANES)
        for s in range(STEPS):
            tokens = slice(s * groups, (s + 1) * groups)
            wide_ref[pl.ds(k * STEPS + s, groups, stride=PIECE), :] = here_ref[
                tokens, columns
            ] + came_ref[tokens, columns].astype(f32)
    out_ref[...] = wide_ref[...].astype(bf16)


def output_kernel(own_ref, other_ref, out_ref, rows_ref):
    steps, width = out_ref.shape
    lower = lax.axis_index("ep") == 0
    own, other = own_ref[...], other_ref[...]
    rows_ref[:PIECE, :] = jnp.where(lower, own, other)
    rows_ref[HALF_ROWS : HALF_ROWS + PIECE, :] = jnp.where(lower, other, own)
    for k in range(width // LANES):
        out_ref[:, k * LANES : (k + 1) * LANES] = rows_ref[k * steps : (k + 1) * steps, :].astype(
            bf16
        )


def on_device(
    queries,
    new_keys,
    new_values,
    cache_keys,
    cache_values,
    lengths,
    residual,
    out_weight,
    norm_gain,
    router_weight,
    routes,
    expert_gate,
    expert_up,
    expert_down,
):
    groups = lax.axis_size("grp")
    steps, _, query_width = queries.shape
    rows = steps * query_width // HD
    struct = jax.ShapeDtypeStruct
    token_count = groups * steps
    width = residual.shape[2]
    kv_width = cache_keys.shape[2]
    cached = cache_keys.shape[1]
    mask = call(mask_kernel, struct((8, cached), f32), (lengths,), [SMEM], beside=3)
    partial = call(
        attention_kernel,
        struct((rows, 2 * HD), bf16),
        (
            mask,
            queries.reshape(steps, query_width),
            cache_keys.reshape(cached, kv_width),
            cache_values.reshape(cached, kv_width),
            new_keys.reshape(steps, kv_width),
            new_values.reshape(steps, kv_width),
        ),
        [VMEM] * 6,
        [pltpu.VMEM((rows, HD), f32)],
        beside=2,
    )
    square = struct((PAIRS, LANES, LANES), bf16)
    residual_rows, routes_row, tables, turned = call(
        rows_kernel,
        (struct((2 * PIECE, LANES), f32), struct((2, LANES), jnp.int32), square, square),
        (residual.reshape(steps, width), routes.transpose(0, 2, 1)),
        [VMEM] * 2,
    )
    other = lax.ppermute(partial, "tp", swap)
    attended = call(
        join_kernel,
        struct((steps, query_width), bf16),
        (partial, other),
        [VMEM] * 2,
        [pltpu.VMEM((rows, HD), f32)],
        beside=2,
    )
    away, here = (
        call(
            functools.partial(project_kernel, is_away),
            struct((PIECE, LANES), kind),
            (attended, out_weight),
            [VMEM] * 2,
            [pltpu.VMEM((PIECE, LANES), f32)],
            beside=beside,
        )
        for is_away, kind, beside in ((True, bf16, 20), (False, f32, 3))
    )
    came = lax.ppermute(away, "ep", swap)
    state, sent_state = call(
        state_kernel,
        (struct((PIECE, LANES), f32), struct((groups * PIECE, LANES), bf16)),
        (residual_rows, here, came),
        [VMEM] * 3,
        [pltpu.VMEM((groups * PIECE, LANES), f32)],
    )
    own_state = lax.all_to_all(
        sent_state.reshape(groups, PIECE, LANES), "grp", 0, 0
    ).reshape(groups * PIECE, LANES)
    other_state = lax.ppermute(own_state, "ep", swap)
    gain = norm_gain.reshape(1, -1)
    router = router_weight.T
    expert_width = expert_gate.shape[2]
    hidden_width = 2 * expert_width
    part = (token_count, width // (2 * HALF_PARTS))
    wide = pltpu.VMEM((groups * PIECE, LANES), f32)
    sums = pltpu.VMEM((4, token_count, expert_width), f32)
    both = pltpu.VMEM((2, LANES, hidden_width), bf16)
    own_terms, squares, logits = call(
        own_half_kernel,
        (
            struct((4 * PAIRS, token_count, expert_width), f32),
            struct((token_count, LANES), f32),
            struct((E, token_count), f32),
        ),
        (own_state, gain, router, expert_gate, expert_up),
        [VMEM] * 5,
        [pltpu.VMEM(part, bf16)] * HALF_PARTS + [wide, sums],
    )
    hidden, *scaled = call(
        hidden_kernel,
        (
            struct((2 * CAP + EXTRA, hidden_width), bf16),
            *[struct(part, bf16)] * HALF_PARTS,
        ),
        (
            other_state,
            gain,
            router,
            tables,
            expert_gate,
            expert_up,
            own_terms,
            squares,
            logits,
        ),
        [VMEM] * 9,
        [wide, sums, both],
    )
    other_hidden = lax.ppermute(hidden, "tp", swap)
    hidden_rest = call(
        hidden_rest_kernel,
        struct((2 * CAP, hidden_width), bf16),
        (*scaled, tables, expert_gate, expert_up, own_terms),
        [VMEM] * (HALF_PARTS + 4),
        [sums, both],
    )
    other_hidden_rest = lax.ppermute(hidden_rest, "tp", swap)
    side = pltpu.VMEM((LANES, hidden_width), bf16)
    down_terms, factors = call(
        down_kernel,
        (struct((token_count, width), f32), struct((2 * CAP, LANES), f32)),
        (hidden, other_hidden, routes_row, tables, turned, expert_down),
        [VMEM] * 6,
        [side],
        limit=8,
    )
    half = width // 2
    away, spread = call(
        down_away_kernel,
        (struct((token_count, half), bf16), struct((token_count, hidden_width), bf16)),
        (hidden_rest, other_hidden_rest, down_terms, factors, turned, expert_down),
        [VMEM] * 6,
        [side],
    )
    came = lax.ppermute(away, "ep", swap)
    here = call(
        down_here_kernel,
        struct((token_count, half), f32),
        (spread, down_terms, expert_down),
        [VMEM] * 3,
    )
    sent = call(
        send_kernel,
        struct((groups * PIECE, LANES), bf16),
        (here, came),
        [VMEM] * 2,
        [wide],
    )
    received = lax.all_to_all(sent.reshape(groups, PIECE, LANES), "grp", 0, 0)
    summed = state + jnp.sum(received.astype(f32), axis=0)
    other_summed = lax.ppermute(summed, "ep", swap)
    mixed = call(
        output_kernel,
        struct((steps, width), bf16),
        (summed, other_summed),
        [VMEM] * 2,
        [pltpu.VMEM((2 * PIECE, LANES), f32)],
    )
    return mixed[:, None]


def solution(mesh):
    in_specs = (
        P(None, "grp", "ep"),
        P(None, "grp", "ep"),
        P(None, "grp", "ep"),
        P("grp", "tp", "ep"),
        P("grp", "tp", "ep"),
        P("grp"),
        P(None, "grp", "tp"),
        P("ep", "tp"),
        P("tp"),
        P("tp", None),
        P(),
        P("ep", "tp", "grp"),
        P("ep", "tp", "grp"),
        P("ep", "grp", "tp"),
    )
    out_specs = P(None, "grp", "tp")
    return jax.shard_map(
        on_device, mesh=mesh, in_specs=in_specs, out_specs=out_specs, check_vma=False
    )
```

```python
import functools

import jax
import jax.numpy as jnp
from jax import lax
from jax.experimental import pallas as pl
from jax.experimental.pallas import tpu as pltpu
from jax.sharding import PartitionSpec as P

D = 6144
HD = 128
E = 8
CAP = 48
PAIRS = 2
STEPS = 3
HALF_PARTS = 2
HALF_ROWS = 36
PIECE = 40
EXTRA = 8
LANES = 128

far_below = -1e30
epsilon = 1e-05
VMEM = pl.BlockSpec(memory_space=pltpu.VMEM)
SMEM = pl.BlockSpec(memory_space=pltpu.SMEM)
swap = [(0, 1), (1, 0)]
f32 = jnp.float32
bf16 = jnp.bfloat16


def call(kernel, out, operands, specs, scratch=(), limit=4, beside=0):
    return pl.pallas_call(
        kernel,
        out_shape=out,
        in_specs=specs,
        out_specs=jax.tree.map(lambda _: VMEM, out),
        scratch_shapes=scratch,
        compiler_params=pltpu.CompilerParams(vmem_limit_bytes=limit * 2**20),
        cost_estimate=pl.CostEstimate(
            flops=beside * 10**9, bytes_accessed=0, transcendentals=0
        )
        if beside
        else None,
    )(*operands)


def iota(shape, dim):
    return lax.broadcasted_iota(jnp.int32, shape, dim)


def pieces(value):
    high = value.astype(bf16).astype(f32)
    rest = value - high
    middle = rest.astype(bf16).astype(f32)
    return high, middle, rest - middle


def mask_kernel(length_ref, out_ref):
    cached = out_ref.shape[1]
    place = iota(out_ref.shape, 1) + lax.axis_index("tp") * cached
    out_ref[...] = jnp.where(place < length_ref[0], 1.0, 0.0)


def rows_kernel(residual_ref, routes_ref, rows_ref, routes_row_ref, tables_ref, turned_ref):
    steps, width = residual_ref.shape
    groups = routes_ref.shape[2]
    for k in range(width // LANES):
        rows_ref[k * steps : (k + 1) * steps, :] = residual_ref[
            :, k * LANES : (k + 1) * LANES
        ].astype(f32)
    used = steps * width // LANES
    rows_ref[used:, :] = jnp.zeros((rows_ref.shape[0] - used, LANES), f32)
    routes_row_ref[...] = jnp.full(routes_row_ref.shape, -1, jnp.int32)
    for s in range(steps):
        routes_row_ref[:, s * groups : (s + 1) * groups] = routes_ref[s]
    count = E // 2
    wanted = iota((E, LANES), 0) + lax.axis_index("ep") * count
    ones = jnp.where(
        (routes_row_ref[0:1, :] == wanted) | (routes_row_ref[1:2, :] == wanted), 1.0, 0.0
    )
    earlier = jnp.where(iota((LANES, LANES), 0) < iota((LANES, LANES), 1), 1.0, 0.0)
    place = jnp.dot(
        ones.astype(bf16), earlier.astype(bf16), preferred_element_type=f32
    ).astype(jnp.int32)
    slot = iota((CAP, LANES), 0)
    for pair in range(PAIRS):
        table = jnp.concatenate(
            [
                jnp.where(place[e : e + 1, :] == slot, ones[e : e + 1, :], 0.0)
                for e in (2 * pair, 2 * pair + 1)
            ]
            + [jnp.zeros((LANES - 2 * CAP, LANES), f32)],
            axis=0,
        )
        tables_ref[pair] = table.astype(bf16)
        turned_ref[pair] = table.T.astype(bf16)


def attention_kernel(
    mask_ref, query_ref, key_ref, value_ref, new_key_ref, new_value_ref, out_ref, rows_ref
):
    steps = query_ref.shape[0]
    heads = query_ref.shape[1] // HD
    kv = key_ref.shape[1] // HD
    rows = heads * steps
    per_kv = rows // kv
    part = lax.axis_index("tp")
    for h in range(heads):
        rows_ref[h * steps : (h + 1) * steps, :] = query_ref[:, h * HD : (h + 1) * HD].astype(f32)
    query = rows_ref[...]
    row = iota((rows, 1), 0)
    owner = [(row >= k * per_kv) & (row < (k + 1) * per_kv) for k in range(kv)]
    step = row % steps
    scale = HD ** (-0.5)
    spread = jnp.concatenate(
        [jnp.where(owner[k], query, 0.0).astype(bf16) for k in range(kv)], axis=1
    )
    scores = (
        lax.dot_general(
            spread, key_ref[...], (((1,), (1,)), ((), ())), preferred_element_type=f32
        )
        * scale
    )
    allowed = mask_ref[0:1, :] > 0.0
    scores = jnp.where(allowed, scores, far_below)
    new_key = new_key_ref[...].astype(f32)

    def chosen(wide, t):
        out = jnp.zeros((rows, HD), f32)
        for k in range(kv):
            out = jnp.where(owner[k], wide[t : t + 1, k * HD : (k + 1) * HD], out)
        return out

    fresh_ok = [(step >= t) & (part == 0) for t in range(steps)]
    fresh = [
        jnp.where(
            fresh_ok[t],
            jnp.sum(query * chosen(new_key, t), axis=1, keepdims=True) * scale,
            far_below,
        )
        for t in range(steps)
    ]
    highest = jnp.max(scores, axis=1, keepdims=True)
    for t in range(steps):
        highest = jnp.maximum(highest, fresh[t])
    exponent = jnp.where(allowed, jnp.exp(scores - highest), 0.0)
    totals = jnp.sum(exponent, axis=1, keepdims=True)
    new_value = new_value_ref[...].astype(f32)
    wide = jnp.dot(exponent.astype(bf16), value_ref[...], preferred_element_type=f32)
    weighted = jnp.zeros((rows, HD), f32)
    for k in range(kv):
        weighted = jnp.where(owner[k], wide[:, k * HD : (k + 1) * HD], weighted)
    for t in range(steps):
        term = jnp.where(fresh_ok[t], jnp.exp(fresh[t] - highest), 0.0)
        totals = totals + term
        weighted = weighted + term.astype(bf16).astype(f32) * chosen(new_value, t)
    present = totals > 0.0
    safe = jnp.where(present, totals, 1.0)
    out_ref[:, :HD] = (weighted / safe).astype(bf16)
    tail = pieces(highest) + pieces(totals)
    lane = iota((rows, LANES), 1)
    row_tail = jnp.zeros((rows, LANES), f32)
    for i, piece in enumerate(tail):
        row_tail = jnp.where(lane == i, piece, row_tail)
    out_ref[:, HD:] = row_tail.astype(bf16)


def join_kernel(own_ref, other_ref, attended_ref, rows_ref):
    steps = attended_ref.shape[0]
    heads = own_ref.shape[0] // steps

    def read(ref):
        tail = ref[:, HD:].astype(f32)
        highest = tail[:, 0:1] + tail[:, 1:2] + tail[:, 2:3]
        totals = tail[:, 3:4] + tail[:, 4:5] + tail[:, 5:6]
        return ref[:, :HD].astype(f32), highest, totals

    own, own_highest, own_totals = read(own_ref)
    other, other_highest, other_totals = read(other_ref)
    top = jnp.maximum(own_highest, other_highest)
    own_factor = own_totals * jnp.exp(own_highest - top)
    other_factor = other_totals * jnp.exp(other_highest - top)
    rows_ref[...] = (own * own_factor + other * other_factor) / (own_factor + other_factor)
    attended_ref[...] = jnp.concatenate(
        [rows_ref[h * steps : (h + 1) * steps, :] for h in range(heads)], axis=1
    ).astype(bf16)


def project_kernel(away, attended_ref, weight_ref, out_ref, rows_ref):
    steps = attended_ref.shape[0]
    width = weight_ref.shape[1] // 2
    half = lax.axis_index("ep")
    if away:
        half = 1 - half
    columns = pl.ds(pl.multiple_of(half * width, LANES), width)
    terms = jnp.dot(attended_ref[...], weight_ref[:, columns], preferred_element_type=f32)
    used = steps * width // LANES
    rows_ref[used:, :] = jnp.zeros((rows_ref.shape[0] - used, LANES), f32)
    for k in range(width // LANES):
        rows_ref[k * steps : (k + 1) * steps, :] = terms[:, k * LANES : (k + 1) * LANES]
    out_ref[...] = rows_ref[...].astype(out_ref.dtype)


def state_kernel(residual_ref, here_ref, came_ref, state_ref, sent_ref, wide_ref):
    residual = jnp.where(
        lax.axis_index("ep") == 0,
        residual_ref[:PIECE, :],
        residual_ref[HALF_ROWS : HALF_ROWS + PIECE, :],
    )
    state = (residual + (here_ref[...] + came_ref[...].astype(f32))).astype(bf16).astype(f32)
    state_ref[...] = state
    for g in range(wide_ref.shape[0] // PIECE):
        wide_ref[g * PIECE : (g + 1) * PIECE, :] = state
    sent_ref[...] = wide_ref[...].astype(bf16)


def scale_half(first, state_ref, gain_ref, scaled_refs, wide_ref):
    part = scaled_refs[0].shape[1]
    groups = state_ref.shape[0] // PIECE
    wide_ref[...] = state_ref[...].astype(f32)
    squares = [jnp.zeros((groups, LANES), f32) for _ in range(STEPS)]
    for k in range(len(scaled_refs) * part // LANES):
        gain = gain_ref[:, pl.ds(pl.multiple_of(first + k * LANES, LANES), LANES)]
        scaled_ref = scaled_refs[k * LANES // part]
        column = k * LANES % part
        for s in range(STEPS):
            block = wide_ref[pl.ds(k * STEPS + s, groups, stride=PIECE), :]
            squares[s] = squares[s] + block * block
            scaled_ref[s * groups : (s + 1) * groups, column : column + LANES] = (
                block * gain
            ).astype(bf16)
    return jnp.concatenate(squares, axis=0)


def route_half(first, router_ref, scaled_refs):
    part = scaled_refs[0].shape[1]
    return sum(
        lax.dot_general(
            router_ref[:, pl.ds(pl.multiple_of(first + n * part, LANES), part)],
            ref[...],
            (((1,), (1,)), ((), ())),
            preferred_element_type=f32,
        )
        for n, ref in enumerate(scaled_refs)
    )


def add_half(first, pair, scaled_refs, gate_ref, up_ref, before_ref, sums_ref, put):
    part = scaled_refs[0].shape[1]
    last = len(scaled_refs) - 1
    for n, scaled_ref in enumerate(scaled_refs):
        scaled = scaled_ref[...]
        depth = pl.ds(pl.multiple_of(first + n * part, LANES), part)
        for i in range(2):
            for j, weight_ref in enumerate((gate_ref, up_ref)):
                terms = jnp.dot(
                    scaled, weight_ref[2 * pair + i, depth, :], preferred_element_type=f32
                )
                if n > 0:
                    terms = terms + sums_ref[2 * i + j]
                elif before_ref is not None:
                    terms = terms + before_ref[4 * pair + 2 * i + j]
                if n < last:
                    sums_ref[2 * i + j] = terms
                else:
                    put(i, j, terms)


def own_half_kernel(
    state_ref, gain_ref, router_ref, gate_ref, up_ref, terms_ref, square_ref, logits_ref, *refs
):
    *scaled_refs, wide_ref, sums_ref = refs
    first = lax.axis_index("ep") * (len(scaled_refs) * scaled_refs[0].shape[1])
    square_ref[...] = scale_half(first, state_ref, gain_ref, scaled_refs, wide_ref)
    for pair in range(PAIRS):

        def put(i, j, terms, pair=pair):
            terms_ref[4 * pair + 2 * i + j] = terms

        add_half(first, pair, scaled_refs, gate_ref, up_ref, None, sums_ref, put)
    logits_ref[...] = route_half(first, router_ref, scaled_refs)


def pack_pair(
    first, pair, scaled_refs, tables_ref, gate_ref, up_ref, terms_ref, out_ref, sums_ref, both_ref
):
    tokens = scaled_refs[0].shape[0]
    width = gate_ref.shape[2]
    both_ref[:, tokens:, :] = jnp.zeros((2, LANES - tokens, 2 * width), bf16)

    def put(i, j, terms):
        both_ref[i, :tokens, j * width : (j + 1) * width] = terms.astype(bf16)

    add_half(first, pair, scaled_refs, gate_ref, up_ref, terms_ref, sums_ref, put)
    for i in range(2):
        out_ref[i * CAP : (i + 1) * CAP, :] = jnp.dot(
            tables_ref[pair, i * CAP : (i + 1) * CAP, :],
            both_ref[i],
            preferred_element_type=f32,
        ).astype(bf16)


def hidden_kernel(
    state_ref,
    gain_ref,
    router_ref,
    tables_ref,
    gate_ref,
    up_ref,
    terms_ref,
    square_ref,
    logits_ref,
    out_ref,
    *refs,
):
    *scaled_refs, wide_ref, sums_ref, both_ref = refs
    tokens = scaled_refs[0].shape[0]
    first = (1 - lax.axis_index("ep")) * (len(scaled_refs) * scaled_refs[0].shape[1])
    squares = square_ref[...] + scale_half(first, state_ref, gain_ref, scaled_refs, wide_ref)
    pack_pair(
        first, 0, scaled_refs, tables_ref, gate_ref, up_ref, terms_ref, out_ref, sums_ref, both_ref
    )
    square = jnp.sum(squares, axis=1, keepdims=True)
    diagonal = iota((tokens, LANES), 0) == iota((tokens, LANES), 1)
    square = jnp.sum(jnp.where(diagonal, square, 0.0), axis=0, keepdims=True)
    router = logits_ref[...] + route_half(first, router_ref, scaled_refs)
    router = jnp.concatenate([router, jnp.zeros((E, LANES - tokens), f32)], axis=1)
    high, middle, _ = pieces(router)
    square_high, square_middle, _ = pieces(square)
    line = iota((E, LANES), 0)
    extra = jnp.concatenate(
        [
            high,
            middle,
            jnp.where(line == 0, square_high, jnp.where(line == 1, square_middle, 0.0)),
            jnp.zeros((E, LANES), f32),
        ],
        axis=1,
    )
    out_ref[2 * CAP :, :] = extra.astype(bf16)


def hidden_rest_kernel(*refs):
    *scaled_refs, tables_ref, gate_ref, up_ref, terms_ref, out_ref, sums_ref, both_ref = refs
    first = (1 - lax.axis_index("ep")) * (len(scaled_refs) * scaled_refs[0].shape[1])
    pack_pair(
        first, 1, scaled_refs, tables_ref, gate_ref, up_ref, terms_ref, out_ref, sums_ref, both_ref
    )


def spread_pair(own_ref, other_ref, factors, turned, side_ref, tokens):
    width = side_ref.shape[1] // 2
    side_ref[...] = jnp.zeros(side_ref.shape, bf16)
    both = own_ref[: 2 * CAP, :].astype(f32) + other_ref[: 2 * CAP, :].astype(f32)
    both = both * factors[:, 0:1]
    gate, up = both[:, :width], both[:, width:]
    activated = (gate / (1.0 + jnp.exp(-gate)) * up).astype(bf16).astype(f32)
    weighted = (activated * factors[:, 1:2]).astype(bf16)
    for i in range(2):
        side_ref[i * CAP : (i + 1) * CAP, i * width : (i + 1) * width] = weighted[
            i * CAP : (i + 1) * CAP, :
        ]
    return jnp.dot(turned[:tokens, :], side_ref[...], preferred_element_type=f32).astype(bf16)


def down_kernel(
    own_ref, other_ref, routes_ref, tables_ref, turned_ref, down_ref, terms_ref, factors_ref, side_ref
):
    tokens = terms_ref.shape[0]
    width = down_ref.shape[1]
    tail = own_ref[2 * CAP :, :].astype(f32) + other_ref[2 * CAP :, :].astype(f32)
    square = tail[0:1, 2 * LANES : 3 * LANES] + tail[1:2, 2 * LANES : 3 * LANES]
    inverse = lax.rsqrt(square / D + epsilon)
    logits = (tail[:E, :LANES] + tail[:E, LANES : 2 * LANES]) * inverse
    every = iota((E, LANES), 0)
    picked = [
        jnp.sum(jnp.where(routes_ref[c : c + 1, :] == every, logits, 0.0), axis=0, keepdims=True)
        for c in range(2)
    ]
    top = jnp.maximum(picked[0], picked[1])
    raised = [jnp.exp(p - top) for p in picked]
    total = raised[0] + raised[1]
    shares = [r / total for r in raised]
    first = lax.axis_index("ep") * (2 * PAIRS)

    def factors_of(pair):
        slots = []
        for i in range(2):
            share = jnp.zeros((1, LANES), f32)
            for c in range(2):
                share = share + jnp.where(
                    routes_ref[c : c + 1, :] == first + 2 * pair + i, shares[c], 0.0
                )
            slots.append(jnp.broadcast_to(share, (CAP, LANES)))
        table = tables_ref[pair, : 2 * CAP, :].astype(f32)
        slot_inverse = jnp.sum(table * inverse, axis=1, keepdims=True)
        slot_share = jnp.sum(table * jnp.concatenate(slots, axis=0), axis=1, keepdims=True)
        return jnp.where(iota((2 * CAP, LANES), 1) == 0, slot_inverse, slot_share)

    factors_ref[...] = factors_of(1)
    mixed = spread_pair(own_ref, other_ref, factors_of(0), turned_ref[0], side_ref, tokens)
    terms_ref[...] = sum(
        jnp.dot(
            mixed[:, e * width : (e + 1) * width], down_ref[e], preferred_element_type=f32
        )
        for e in range(2)
    )


def half_terms(first, mixed, terms_ref, down_ref, width, put):
    depth = down_ref.shape[1]
    chunk = 4 * LANES
    for n in range(width // chunk):
        columns = pl.ds(pl.multiple_of(first + n * chunk, LANES), chunk)
        terms = terms_ref[:, columns]
        for i in range(2):
            terms = terms + jnp.dot(
                mixed[:, i * depth : (i + 1) * depth],
                down_ref[2 + i, :, columns],
                preferred_element_type=f32,
            )
        put(n * chunk, terms)


def down_away_kernel(
    own_ref, other_ref, terms_ref, factors_ref, turned_ref, down_ref, away_ref, mixed_ref, side_ref
):
    tokens, width = away_ref.shape
    mixed = spread_pair(own_ref, other_ref, factors_ref[...], turned_ref[1], side_ref, tokens)
    mixed_ref[...] = mixed

    def put(column, terms):
        away_ref[:, column : column + terms.shape[1]] = terms.astype(bf16)

    first = (1 - lax.axis_index("ep")) * width
    half_terms(first, mixed, terms_ref, down_ref, width, put)


def down_here_kernel(mixed_ref, terms_ref, down_ref, here_ref):
    width = here_ref.shape[1]

    def put(column, terms):
        here_ref[:, column : column + terms.shape[1]] = terms

    half_terms(lax.axis_index("ep") * width, mixed_ref[...], terms_ref, down_ref, width, put)


def send_kernel(here_ref, came_ref, out_ref, wide_ref):
    groups = here_ref.shape[0] // STEPS
    blocks = here_ref.shape[1] // LANES
    wide_ref[...] = jnp.zeros(wide_ref.shape, f32)
    for k in range(blocks):
        columns = slice(k * LANES, (k + 1) * LANES)
        for s in range(STEPS):
            tokens = slice(s * groups, (s + 1) * groups)
            wide_ref[pl.ds(k * STEPS + s, groups, stride=PIECE), :] = here_ref[
                tokens, columns
            ] + came_ref[tokens, columns].astype(f32)
    out_ref[...] = wide_ref[...].astype(bf16)


def output_kernel(own_ref, other_ref, out_ref, rows_ref):
    steps, width = out_ref.shape
    lower = lax.axis_index("ep") == 0
    own, other = own_ref[...], other_ref[...]
    rows_ref[:PIECE, :] = jnp.where(lower, own, other)
    rows_ref[HALF_ROWS : HALF_ROWS + PIECE, :] = jnp.where(lower, other, own)
    for k in range(width // LANES):
        out_ref[:, k * LANES : (k + 1) * LANES] = rows_ref[k * steps : (k + 1) * steps, :].astype(
            bf16
        )


def on_device(
    queries,
    new_keys,
    new_values,
    cache_keys,
    cache_values,
    lengths,
    residual,
    out_weight,
    norm_gain,
    router_weight,
    routes,
    expert_gate,
    expert_up,
    expert_down,
):
    groups = lax.axis_size("grp")
    steps, _, query_width = queries.shape
    rows = steps * query_width // HD
    struct = jax.ShapeDtypeStruct
    token_count = groups * steps
    width = residual.shape[2]
    kv_width = cache_keys.shape[2]
    cached = cache_keys.shape[1]
    mask = call(mask_kernel, struct((8, cached), f32), (lengths,), [SMEM], beside=3)
    partial = call(
        attention_kernel,
        struct((rows, 2 * HD), bf16),
        (
            mask,
            queries.reshape(steps, query_width),
            cache_keys.reshape(cached, kv_width),
            cache_values.reshape(cached, kv_width),
            new_keys.reshape(steps, kv_width),
            new_values.reshape(steps, kv_width),
        ),
        [VMEM] * 6,
        [pltpu.VMEM((rows, HD), f32)],
        beside=2,
    )
    square = struct((PAIRS, LANES, LANES), bf16)
    residual_rows, routes_row, tables, turned = call(
        rows_kernel,
        (struct((2 * PIECE, LANES), f32), struct((2, LANES), jnp.int32), square, square),
        (residual.reshape(steps, width), routes.transpose(0, 2, 1)),
        [VMEM] * 2,
    )
    other = lax.ppermute(partial, "tp", swap)
    attended = call(
        join_kernel,
        struct((steps, query_width), bf16),
        (partial, other),
        [VMEM] * 2,
        [pltpu.VMEM((rows, HD), f32)],
        beside=2,
    )
    away, here = (
        call(
            functools.partial(project_kernel, is_away),
            struct((PIECE, LANES), kind),
            (attended, out_weight),
            [VMEM] * 2,
            [pltpu.VMEM((PIECE, LANES), f32)],
            beside=beside,
        )
        for is_away, kind, beside in ((True, bf16, 20), (False, f32, 3))
    )
    came = lax.ppermute(away, "ep", swap)
    state, sent_state = call(
        state_kernel,
        (struct((PIECE, LANES), f32), struct((groups * PIECE, LANES), bf16)),
        (residual_rows, here, came),
        [VMEM] * 3,
        [pltpu.VMEM((groups * PIECE, LANES), f32)],
    )
    own_state = lax.all_to_all(
        sent_state.reshape(groups, PIECE, LANES), "grp", 0, 0
    ).reshape(groups * PIECE, LANES)
    other_state = lax.ppermute(own_state, "ep", swap)
    gain = norm_gain.reshape(1, -1)
    router = router_weight.T
    expert_width = expert_gate.shape[2]
    hidden_width = 2 * expert_width
    part = (token_count, width // (2 * HALF_PARTS))
    wide = pltpu.VMEM((groups * PIECE, LANES), f32)
    sums = pltpu.VMEM((4, token_count, expert_width), f32)
    both = pltpu.VMEM((2, LANES, hidden_width), bf16)
    own_terms, squares, logits = call(
        own_half_kernel,
        (
            struct((4 * PAIRS, token_count, expert_width), f32),
            struct((token_count, LANES), f32),
            struct((E, token_count), f32),
        ),
        (own_state, gain, router, expert_gate, expert_up),
        [VMEM] * 5,
        [pltpu.VMEM(part, bf16)] * HALF_PARTS + [wide, sums],
    )
    hidden, *scaled = call(
        hidden_kernel,
        (
            struct((2 * CAP + EXTRA, hidden_width), bf16),
            *[struct(part, bf16)] * HALF_PARTS,
        ),
        (
            other_state,
            gain,
            router,
            tables,
            expert_gate,
            expert_up,
            own_terms,
            squares,
            logits,
        ),
        [VMEM] * 9,
        [wide, sums, both],
    )
    other_hidden = lax.ppermute(hidden, "tp", swap)
    hidden_rest = call(
        hidden_rest_kernel,
        struct((2 * CAP, hidden_width), bf16),
        (*scaled, tables, expert_gate, expert_up, own_terms),
        [VMEM] * (HALF_PARTS + 4),
        [sums, both],
    )
    other_hidden_rest = lax.ppermute(hidden_rest, "tp", swap)
    side = pltpu.VMEM((LANES, hidden_width), bf16)
    down_terms, factors = call(
        down_kernel,
        (struct((token_count, width), f32), struct((2 * CAP, LANES), f32)),
        (hidden, other_hidden, routes_row, tables, turned, expert_down),
        [VMEM] * 6,
        [side],
        limit=8,
    )
    half = width // 2
    away, spread = call(
        down_away_kernel,
        (struct((token_count, half), bf16), struct((token_count, hidden_width), bf16)),
        (hidden_rest, other_hidden_rest, down_terms, factors, turned, expert_down),
        [VMEM] * 6,
        [side],
    )
    came = lax.ppermute(away, "ep", swap)
    here = call(
        down_here_kernel,
        struct((token_count, half), f32),
        (spread, down_terms, expert_down),
        [VMEM] * 3,
    )
    sent = call(
        send_kernel,
        struct((groups * PIECE, LANES), bf16),
        (here, came),
        [VMEM] * 2,
        [wide],
    )
    received = lax.all_to_all(sent.reshape(groups, PIECE, LANES), "grp", 0, 0)
    summed = state + jnp.sum(received.astype(f32), axis=0)
    other_summed = lax.ppermute(summed, "ep", swap)
    mixed = call(
        output_kernel,
        struct((steps, width), bf16),
        (summed, other_summed),
        [VMEM] * 2,
        [pltpu.VMEM((2 * PIECE, LANES), f32)],
    )
    return mixed[:, None]


def solution(mesh):
    in_specs = (
        P(None, "grp", "ep"),
        P(None, "grp", "ep"),
        P(None, "grp", "ep"),
        P("grp", "tp", "ep"),
        P("grp", "tp", "ep"),
        P("grp"),
        P(None, "grp", "tp"),
        P("ep", "tp"),
        P("tp"),
        P("tp", None),
        P(),
        P("ep", "tp", "grp"),
        P("ep", "tp", "grp"),
        P("ep", "grp", "tp"),
    )
    out_specs = P(None, "grp", "tp")
    return jax.shard_map(
        on_device, mesh=mesh, in_specs=in_specs, out_specs=out_specs, check_vma=False
    )
```

```python
import functools

import jax
import jax.numpy as jnp
from jax import lax
from jax.experimental import pallas as pl
from jax.experimental.pallas import tpu as pltpu
from jax.sharding import PartitionSpec as P

D = 6144
HD = 128
E = 8
CAP = 48
PAIRS = 2
STEPS = 3
HALF_PARTS = 2
HALF_ROWS = 36
PIECE = 40
EXTRA = 16
LANES = 128

far_below = -1e30
epsilon = 1e-05
VMEM = pl.BlockSpec(memory_space=pltpu.VMEM)
SMEM = pl.BlockSpec(memory_space=pltpu.SMEM)
swap = [(0, 1), (1, 0)]
f32 = jnp.float32
bf16 = jnp.bfloat16


def call(kernel, out, operands, specs, scratch=(), limit=4, beside=0):
    return pl.pallas_call(
        kernel,
        out_shape=out,
        in_specs=specs,
        out_specs=jax.tree.map(lambda _: VMEM, out),
        scratch_shapes=scratch,
        compiler_params=pltpu.CompilerParams(vmem_limit_bytes=limit * 2**20),
        cost_estimate=pl.CostEstimate(
            flops=beside * 10**9, bytes_accessed=0, transcendentals=0
        )
        if beside
        else None,
    )(*operands)


def iota(shape, dim):
    return lax.broadcasted_iota(jnp.int32, shape, dim)


def pieces(value):
    high = value.astype(bf16).astype(f32)
    rest = value - high
    middle = rest.astype(bf16).astype(f32)
    return high, middle, rest - middle


def mask_kernel(length_ref, out_ref):
    cached = out_ref.shape[1]
    place = iota(out_ref.shape, 1) + lax.axis_index("tp") * cached
    out_ref[...] = jnp.where(place < length_ref[0], 1.0, 0.0)


def rows_kernel(residual_ref, routes_ref, rows_ref, routes_row_ref, tables_ref, turned_ref):
    steps, width = residual_ref.shape
    groups = routes_ref.shape[2]
    for k in range(width // LANES):
        rows_ref[k * steps : (k + 1) * steps, :] = residual_ref[
            :, k * LANES : (k + 1) * LANES
        ].astype(f32)
    used = steps * width // LANES
    rows_ref[used:, :] = jnp.zeros((rows_ref.shape[0] - used, LANES), f32)
    routes_row_ref[...] = jnp.full(routes_row_ref.shape, -1, jnp.int32)
    for s in range(steps):
        routes_row_ref[:, s * groups : (s + 1) * groups] = routes_ref[s]
    count = E // 2
    wanted = iota((E, LANES), 0) + lax.axis_index("ep") * count
    ones = jnp.where(
        (routes_row_ref[0:1, :] == wanted) | (routes_row_ref[1:2, :] == wanted), 1.0, 0.0
    )
    earlier = jnp.where(iota((LANES, LANES), 0) < iota((LANES, LANES), 1), 1.0, 0.0)
    place = jnp.dot(
        ones.astype(bf16), earlier.astype(bf16), preferred_element_type=f32
    ).astype(jnp.int32)
    slot = iota((CAP, LANES), 0)
    for pair in range(PAIRS):
        table = jnp.concatenate(
            [
                jnp.where(place[e : e + 1, :] == slot, ones[e : e + 1, :], 0.0)
                for e in (2 * pair, 2 * pair + 1)
            ]
            + [jnp.zeros((LANES - 2 * CAP, LANES), f32)],
            axis=0,
        )
        tables_ref[pair] = table.astype(bf16)
        turned_ref[pair] = table.T.astype(bf16)


def attention_kernel(
    mask_ref, query_ref, key_ref, value_ref, new_key_ref, new_value_ref, out_ref, rows_ref
):
    steps = query_ref.shape[0]
    heads = query_ref.shape[1] // HD
    kv = key_ref.shape[1] // HD
    rows = heads * steps
    per_kv = rows // kv
    part = lax.axis_index("tp")
    for h in range(heads):
        rows_ref[h * steps : (h + 1) * steps, :] = query_ref[:, h * HD : (h + 1) * HD].astype(f32)
    query = rows_ref[...]
    row = iota((rows, 1), 0)
    owner = [(row >= k * per_kv) & (row < (k + 1) * per_kv) for k in range(kv)]
    step = row % steps
    scale = HD ** (-0.5)
    spread = jnp.concatenate(
        [jnp.where(owner[k], query, 0.0).astype(bf16) for k in range(kv)], axis=1
    )
    scores = (
        lax.dot_general(
            spread, key_ref[...], (((1,), (1,)), ((), ())), preferred_element_type=f32
        )
        * scale
    )
    allowed = mask_ref[0:1, :] > 0.0
    scores = jnp.where(allowed, scores, far_below)
    new_key = new_key_ref[...].astype(f32)

    def chosen(wide, t):
        out = jnp.zeros((rows, HD), f32)
        for k in range(kv):
            out = jnp.where(owner[k], wide[t : t + 1, k * HD : (k + 1) * HD], out)
        return out

    fresh_ok = [(step >= t) & (part == 0) for t in range(steps)]
    fresh = [
        jnp.where(
            fresh_ok[t],
            jnp.sum(query * chosen(new_key, t), axis=1, keepdims=True) * scale,
            far_below,
        )
        for t in range(steps)
    ]
    highest = jnp.max(scores, axis=1, keepdims=True)
    for t in range(steps):
        highest = jnp.maximum(highest, fresh[t])
    exponent = jnp.where(allowed, jnp.exp(scores - highest), 0.0)
    totals = jnp.sum(exponent, axis=1, keepdims=True)
    new_value = new_value_ref[...].astype(f32)
    wide = jnp.dot(exponent.astype(bf16), value_ref[...], preferred_element_type=f32)
    weighted = jnp.zeros((rows, HD), f32)
    for k in range(kv):
        weighted = jnp.where(owner[k], wide[:, k * HD : (k + 1) * HD], weighted)
    for t in range(steps):
        term = jnp.where(fresh_ok[t], jnp.exp(fresh[t] - highest), 0.0)
        totals = totals + term
        weighted = weighted + term.astype(bf16).astype(f32) * chosen(new_value, t)
    present = totals > 0.0
    safe = jnp.where(present, totals, 1.0)
    out_ref[:, :HD] = (weighted / safe).astype(bf16)
    tail = pieces(highest) + pieces(totals)
    lane = iota((rows, LANES), 1)
    row_tail = jnp.zeros((rows, LANES), f32)
    for i, piece in enumerate(tail):
        row_tail = jnp.where(lane == i, piece, row_tail)
    out_ref[:, HD:] = row_tail.astype(bf16)


def join_kernel(own_ref, other_ref, attended_ref, rows_ref):
    steps = attended_ref.shape[0]
    heads = own_ref.shape[0] // steps

    def read(ref):
        tail = ref[:, HD:].astype(f32)
        highest = tail[:, 0:1] + tail[:, 1:2] + tail[:, 2:3]
        totals = tail[:, 3:4] + tail[:, 4:5] + tail[:, 5:6]
        return ref[:, :HD].astype(f32), highest, totals

    own, own_highest, own_totals = read(own_ref)
    other, other_highest, other_totals = read(other_ref)
    top = jnp.maximum(own_highest, other_highest)
    own_factor = own_totals * jnp.exp(own_highest - top)
    other_factor = other_totals * jnp.exp(other_highest - top)
    rows_ref[...] = (own * own_factor + other * other_factor) / (own_factor + other_factor)
    attended_ref[...] = jnp.concatenate(
        [rows_ref[h * steps : (h + 1) * steps, :] for h in range(heads)], axis=1
    ).astype(bf16)


def project_kernel(away, attended_ref, weight_ref, out_ref, rows_ref):
    steps = attended_ref.shape[0]
    width = weight_ref.shape[1] // 2
    half = lax.axis_index("ep")
    if away:
        half = 1 - half
    columns = pl.ds(pl.multiple_of(half * width, LANES), width)
    terms = jnp.dot(attended_ref[...], weight_ref[:, columns], preferred_element_type=f32)
    used = steps * width // LANES
    rows_ref[used:, :] = jnp.zeros((rows_ref.shape[0] - used, LANES), f32)
    for k in range(width // LANES):
        rows_ref[k * steps : (k + 1) * steps, :] = terms[:, k * LANES : (k + 1) * LANES]
    out_ref[...] = rows_ref[...].astype(out_ref.dtype)


def state_kernel(residual_ref, here_ref, came_ref, state_ref, sent_ref, wide_ref):
    residual = jnp.where(
        lax.axis_index("ep") == 0,
        residual_ref[:PIECE, :],
        residual_ref[HALF_ROWS : HALF_ROWS + PIECE, :],
    )
    state = (residual + (here_ref[...] + came_ref[...].astype(f32))).astype(bf16).astype(f32)
    state_ref[...] = state
    for g in range(wide_ref.shape[0] // PIECE):
        wide_ref[g * PIECE : (g + 1) * PIECE, :] = state
    sent_ref[...] = wide_ref[...].astype(bf16)


def scale_half(first, state_ref, gain_ref, scaled_refs, wide_ref):
    part = scaled_refs[0].shape[1]
    groups = state_ref.shape[0] // PIECE
    wide_ref[...] = state_ref[...].astype(f32)
    squares = [jnp.zeros((groups, LANES), f32) for _ in range(STEPS)]
    for k in range(len(scaled_refs) * part // LANES):
        gain = gain_ref[:, pl.ds(pl.multiple_of(first + k * LANES, LANES), LANES)]
        scaled_ref = scaled_refs[k * LANES // part]
        column = k * LANES % part
        for s in range(STEPS):
            block = wide_ref[pl.ds(k * STEPS + s, groups, stride=PIECE), :]
            squares[s] = squares[s] + block * block
            scaled_ref[s * groups : (s + 1) * groups, column : column + LANES] = (
                block * gain
            ).astype(bf16)
    return jnp.concatenate(squares, axis=0)


def route_half(first, router_ref, scaled_refs):
    part = scaled_refs[0].shape[1]
    return sum(
        lax.dot_general(
            router_ref[:, pl.ds(pl.multiple_of(first + n * part, LANES), part)],
            ref[...],
            (((1,), (1,)), ((), ())),
            preferred_element_type=f32,
        )
        for n, ref in enumerate(scaled_refs)
    )


def add_half(first, pair, scaled_refs, gate_ref, up_ref, before_ref, sums_ref, put):
    part = scaled_refs[0].shape[1]
    last = len(scaled_refs) - 1
    for n, scaled_ref in enumerate(scaled_refs):
        scaled = scaled_ref[...]
        depth = pl.ds(pl.multiple_of(first + n * part, LANES), part)
        for i in range(2):
            for j, weight_ref in enumerate((gate_ref, up_ref)):
                terms = jnp.dot(
                    scaled, weight_ref[2 * pair + i, depth, :], preferred_element_type=f32
                )
                if n > 0:
                    terms = terms + sums_ref[2 * i + j]
                elif before_ref is not None:
                    terms = terms + before_ref[4 * pair + 2 * i + j]
                if n < last:
                    sums_ref[2 * i + j] = terms
                else:
                    put(i, j, terms)


def own_half_kernel(
    state_ref, gain_ref, router_ref, gate_ref, up_ref, terms_ref, square_ref, logits_ref, *refs
):
    *scaled_refs, wide_ref, sums_ref = refs
    first = lax.axis_index("ep") * (len(scaled_refs) * scaled_refs[0].shape[1])
    square_ref[...] = scale_half(first, state_ref, gain_ref, scaled_refs, wide_ref)
    for pair in range(PAIRS):

        def put(i, j, terms, pair=pair):
            terms_ref[4 * pair + 2 * i + j] = terms

        add_half(first, pair, scaled_refs, gate_ref, up_ref, None, sums_ref, put)
    logits_ref[...] = route_half(first, router_ref, scaled_refs)


def pack_pair(
    first, pair, scaled_refs, tables_ref, gate_ref, up_ref, terms_ref, out_ref, sums_ref, both_ref
):
    tokens = scaled_refs[0].shape[0]
    width = gate_ref.shape[2]
    both_ref[:, tokens:, :] = jnp.zeros((2, LANES - tokens, 2 * width), bf16)

    def put(i, j, terms):
        both_ref[i, :tokens, j * width : (j + 1) * width] = terms.astype(bf16)

    add_half(first, pair, scaled_refs, gate_ref, up_ref, terms_ref, sums_ref, put)
    for i in range(2):
        out_ref[i * CAP : (i + 1) * CAP, :] = jnp.dot(
            tables_ref[pair, i * CAP : (i + 1) * CAP, :],
            both_ref[i],
            preferred_element_type=f32,
        ).astype(bf16)


def hidden_kernel(
    state_ref,
    gain_ref,
    router_ref,
    tables_ref,
    gate_ref,
    up_ref,
    terms_ref,
    square_ref,
    logits_ref,
    out_ref,
    *refs,
):
    *scaled_refs, wide_ref, sums_ref, both_ref = refs
    tokens = scaled_refs[0].shape[0]
    first = (1 - lax.axis_index("ep")) * (len(scaled_refs) * scaled_refs[0].shape[1])
    squares = square_ref[...] + scale_half(first, state_ref, gain_ref, scaled_refs, wide_ref)
    pack_pair(
        first, 0, scaled_refs, tables_ref, gate_ref, up_ref, terms_ref, out_ref, sums_ref, both_ref
    )
    square = jnp.sum(squares, axis=1, keepdims=True)
    diagonal = iota((tokens, LANES), 0) == iota((tokens, LANES), 1)
    square = jnp.sum(jnp.where(diagonal, square, 0.0), axis=0, keepdims=True)
    router = logits_ref[...] + route_half(first, router_ref, scaled_refs)
    router = jnp.concatenate([router, jnp.zeros((E, LANES - tokens), f32)], axis=1)
    high, middle, _ = pieces(router)
    square_high, square_middle, _ = pieces(square)
    line = iota((E, LANES), 0)
    extra = jnp.concatenate(
        [
            high,
            middle,
            jnp.where(line == 0, square_high, jnp.where(line == 1, square_middle, 0.0)),
            jnp.zeros((E, LANES), f32),
        ],
        axis=1,
    )
    extra = jnp.concatenate([extra, jnp.zeros((EXTRA - E, 4 * LANES), f32)], axis=0)
    out_ref[2 * CAP :, :] = extra.astype(bf16)


def hidden_rest_kernel(*refs):
    *scaled_refs, tables_ref, gate_ref, up_ref, terms_ref, out_ref, sums_ref, both_ref = refs
    first = (1 - lax.axis_index("ep")) * (len(scaled_refs) * scaled_refs[0].shape[1])
    pack_pair(
        first, 1, scaled_refs, tables_ref, gate_ref, up_ref, terms_ref, out_ref, sums_ref, both_ref
    )


def spread_pair(own_ref, other_ref, factors, turned, side_ref, tokens):
    width = side_ref.shape[1] // 2
    side_ref[...] = jnp.zeros(side_ref.shape, bf16)
    both = own_ref[: 2 * CAP, :].astype(f32) + other_ref[: 2 * CAP, :].astype(f32)
    both = both * factors[:, 0:1]
    gate, up = both[:, :width], both[:, width:]
    activated = (gate / (1.0 + jnp.exp(-gate)) * up).astype(bf16).astype(f32)
    weighted = (activated * factors[:, 1:2]).astype(bf16)
    for i in range(2):
        side_ref[i * CAP : (i + 1) * CAP, i * width : (i + 1) * width] = weighted[
            i * CAP : (i + 1) * CAP, :
        ]
    return jnp.dot(turned[:tokens, :], side_ref[...], preferred_element_type=f32).astype(bf16)


def down_kernel(
    own_ref, other_ref, routes_ref, tables_ref, turned_ref, down_ref, terms_ref, factors_ref, side_ref
):
    tokens = terms_ref.shape[0]
    width = down_ref.shape[1]
    tail = own_ref[2 * CAP :, :].astype(f32) + other_ref[2 * CAP :, :].astype(f32)
    square = tail[0:1, 2 * LANES : 3 * LANES] + tail[1:2, 2 * LANES : 3 * LANES]
    inverse = lax.rsqrt(square / D + epsilon)
    logits = (tail[:E, :LANES] + tail[:E, LANES : 2 * LANES]) * inverse
    every = iota((E, LANES), 0)
    picked = [
        jnp.sum(jnp.where(routes_ref[c : c + 1, :] == every, logits, 0.0), axis=0, keepdims=True)
        for c in range(2)
    ]
    top = jnp.maximum(picked[0], picked[1])
    raised = [jnp.exp(p - top) for p in picked]
    total = raised[0] + raised[1]
    shares = [r / total for r in raised]
    first = lax.axis_index("ep") * (2 * PAIRS)

    def factors_of(pair):
        slots = []
        for i in range(2):
            share = jnp.zeros((1, LANES), f32)
            for c in range(2):
                share = share + jnp.where(
                    routes_ref[c : c + 1, :] == first + 2 * pair + i, shares[c], 0.0
                )
            slots.append(jnp.broadcast_to(share, (CAP, LANES)))
        table = tables_ref[pair, : 2 * CAP, :].astype(f32)
        slot_inverse = jnp.sum(table * inverse, axis=1, keepdims=True)
        slot_share = jnp.sum(table * jnp.concatenate(slots, axis=0), axis=1, keepdims=True)
        return jnp.where(iota((2 * CAP, LANES), 1) == 0, slot_inverse, slot_share)

    factors_ref[...] = factors_of(1)
    mixed = spread_pair(own_ref, other_ref, factors_of(0), turned_ref[0], side_ref, tokens)
    terms_ref[...] = sum(
        jnp.dot(
            mixed[:, e * width : (e + 1) * width], down_ref[e], preferred_element_type=f32
        )
        for e in range(2)
    )


def half_terms(first, mixed, terms_ref, down_ref, width, put):
    depth = down_ref.shape[1]
    chunk = 4 * LANES
    for n in range(width // chunk):
        columns = pl.ds(pl.multiple_of(first + n * chunk, LANES), chunk)
        terms = terms_ref[:, columns]
        for i in range(2):
            terms = terms + jnp.dot(
                mixed[:, i * depth : (i + 1) * depth],
                down_ref[2 + i, :, columns],
                preferred_element_type=f32,
            )
        put(n * chunk, terms)


def down_away_kernel(
    own_ref, other_ref, terms_ref, factors_ref, turned_ref, down_ref, away_ref, mixed_ref, side_ref
):
    tokens, width = away_ref.shape
    mixed = spread_pair(own_ref, other_ref, factors_ref[...], turned_ref[1], side_ref, tokens)
    mixed_ref[...] = mixed

    def put(column, terms):
        away_ref[:, column : column + terms.shape[1]] = terms.astype(bf16)

    first = (1 - lax.axis_index("ep")) * width
    half_terms(first, mixed, terms_ref, down_ref, width, put)


def down_here_kernel(mixed_ref, terms_ref, down_ref, here_ref):
    width = here_ref.shape[1]

    def put(column, terms):
        here_ref[:, column : column + terms.shape[1]] = terms

    half_terms(lax.axis_index("ep") * width, mixed_ref[...], terms_ref, down_ref, width, put)


def send_kernel(here_ref, came_ref, out_ref, wide_ref):
    groups = here_ref.shape[0] // STEPS
    blocks = here_ref.shape[1] // LANES
    wide_ref[...] = jnp.zeros(wide_ref.shape, f32)
    for k in range(blocks):
        columns = slice(k * LANES, (k + 1) * LANES)
        for s in range(STEPS):
            tokens = slice(s * groups, (s + 1) * groups)
            wide_ref[pl.ds(k * STEPS + s, groups, stride=PIECE), :] = here_ref[
                tokens, columns
            ] + came_ref[tokens, columns].astype(f32)
    out_ref[...] = wide_ref[...].astype(bf16)


def output_kernel(own_ref, other_ref, out_ref, rows_ref):
    steps, width = out_ref.shape
    lower = lax.axis_index("ep") == 0
    own, other = own_ref[...].astype(f32), other_ref[...].astype(f32)
    rows_ref[:PIECE, :] = jnp.where(lower, own, other)
    rows_ref[HALF_ROWS : HALF_ROWS + PIECE, :] = jnp.where(lower, other, own)
    for k in range(width // LANES):
        out_ref[:, k * LANES : (k + 1) * LANES] = rows_ref[k * steps : (k + 1) * steps, :].astype(
            bf16
        )


def on_device(
    queries,
    new_keys,
    new_values,
    cache_keys,
    cache_values,
    lengths,
    residual,
    out_weight,
    norm_gain,
    router_weight,
    routes,
    expert_gate,
    expert_up,
    expert_down,
):
    groups = lax.axis_size("grp")
    steps, _, query_width = queries.shape
    rows = steps * query_width // HD
    struct = jax.ShapeDtypeStruct
    token_count = groups * steps
    width = residual.shape[2]
    kv_width = cache_keys.shape[2]
    cached = cache_keys.shape[1]
    mask = call(mask_kernel, struct((8, cached), f32), (lengths,), [SMEM], beside=3)
    partial = call(
        attention_kernel,
        struct((rows, 2 * HD), bf16),
        (
            mask,
            queries.reshape(steps, query_width),
            cache_keys.reshape(cached, kv_width),
            cache_values.reshape(cached, kv_width),
            new_keys.reshape(steps, kv_width),
            new_values.reshape(steps, kv_width),
        ),
        [VMEM] * 6,
        [pltpu.VMEM((rows, HD), f32)],
        beside=2,
    )
    square = struct((PAIRS, LANES, LANES), bf16)
    residual_rows, routes_row, tables, turned = call(
        rows_kernel,
        (struct((2 * PIECE, LANES), f32), struct((2, LANES), jnp.int32), square, square),
        (residual.reshape(steps, width), routes.transpose(0, 2, 1)),
        [VMEM] * 2,
    )
    other = lax.ppermute(partial, "tp", swap)
    attended = call(
        join_kernel,
        struct((steps, query_width), bf16),
        (partial, other),
        [VMEM] * 2,
        [pltpu.VMEM((rows, HD), f32)],
        beside=2,
    )
    away, here = (
        call(
            functools.partial(project_kernel, is_away),
            struct((PIECE, LANES), kind),
            (attended, out_weight),
            [VMEM] * 2,
            [pltpu.VMEM((PIECE, LANES), f32)],
            beside=beside,
        )
        for is_away, kind, beside in ((True, bf16, 20), (False, f32, 3))
    )
    came = lax.ppermute(away, "ep", swap)
    state, sent_state = call(
        state_kernel,
        (struct((PIECE, LANES), f32), struct((groups * PIECE, LANES), bf16)),
        (residual_rows, here, came),
        [VMEM] * 3,
        [pltpu.VMEM((groups * PIECE, LANES), f32)],
    )
    own_state = lax.all_to_all(
        sent_state.reshape(groups, PIECE, LANES), "grp", 0, 0
    ).reshape(groups * PIECE, LANES)
    other_state = lax.ppermute(own_state, "ep", swap)
    gain = norm_gain.reshape(1, -1)
    router = router_weight.T
    expert_width = expert_gate.shape[2]
    hidden_width = 2 * expert_width
    part = (token_count, width // (2 * HALF_PARTS))
    wide = pltpu.VMEM((groups * PIECE, LANES), f32)
    sums = pltpu.VMEM((4, token_count, expert_width), f32)
    both = pltpu.VMEM((2, LANES, hidden_width), bf16)
    own_terms, squares, logits = call(
        own_half_kernel,
        (
            struct((4 * PAIRS, token_count, expert_width), f32),
            struct((token_count, LANES), f32),
            struct((E, token_count), f32),
        ),
        (own_state, gain, router, expert_gate, expert_up),
        [VMEM] * 5,
        [pltpu.VMEM(part, bf16)] * HALF_PARTS + [wide, sums],
    )
    hidden, *scaled = call(
        hidden_kernel,
        (
            struct((2 * CAP + EXTRA, hidden_width), bf16),
            *[struct(part, bf16)] * HALF_PARTS,
        ),
        (
            other_state,
            gain,
            router,
            tables,
            expert_gate,
            expert_up,
            own_terms,
            squares,
            logits,
        ),
        [VMEM] * 9,
        [wide, sums, both],
    )
    other_hidden = lax.ppermute(hidden, "tp", swap)
    hidden_rest = call(
        hidden_rest_kernel,
        struct((2 * CAP, hidden_width), bf16),
        (*scaled, tables, expert_gate, expert_up, own_terms),
        [VMEM] * (HALF_PARTS + 4),
        [sums, both],
    )
    other_hidden_rest = lax.ppermute(hidden_rest, "tp", swap)
    side = pltpu.VMEM((LANES, hidden_width), bf16)
    down_terms, factors = call(
        down_kernel,
        (struct((token_count, width), f32), struct((2 * CAP, LANES), f32)),
        (hidden, other_hidden, routes_row, tables, turned, expert_down),
        [VMEM] * 6,
        [side],
        limit=8,
    )
    half = width // 2
    away, spread = call(
        down_away_kernel,
        (struct((token_count, half), bf16), struct((token_count, hidden_width), bf16)),
        (hidden_rest, other_hidden_rest, down_terms, factors, turned, expert_down),
        [VMEM] * 6,
        [side],
    )
    came = lax.ppermute(away, "ep", swap)
    here = call(
        down_here_kernel,
        struct((token_count, half), f32),
        (spread, down_terms, expert_down),
        [VMEM] * 3,
    )
    sent = call(
        send_kernel,
        struct((groups * PIECE, LANES), bf16),
        (here, came),
        [VMEM] * 2,
        [wide],
    )
    received = lax.all_to_all(sent.reshape(groups, PIECE, LANES), "grp", 0, 0)
    summed = (state + jnp.sum(received.astype(f32), axis=0)).astype(bf16)
    other_summed = lax.ppermute(summed, "ep", swap)
    mixed = call(
        output_kernel,
        struct((steps, width), bf16),
        (summed, other_summed),
        [VMEM] * 2,
        [pltpu.VMEM((2 * PIECE, LANES), f32)],
    )
    return mixed[:, None]


def solution(mesh):
    in_specs = (
        P(None, "grp", "ep"),
        P(None, "grp", "ep"),
        P(None, "grp", "ep"),
        P("grp", "tp", "ep"),
        P("grp", "tp", "ep"),
        P("grp"),
        P(None, "grp", "tp"),
        P("ep", "tp"),
        P("tp"),
        P("tp", None),
        P(),
        P("ep", "tp", "grp"),
        P("ep", "tp", "grp"),
        P("ep", "grp", "tp"),
    )
    out_specs = P(None, "grp", "tp")
    return jax.shard_map(
        on_device, mesh=mesh, in_specs=in_specs, out_specs=out_specs, check_vma=False
    )
```
